128 devices in a mesh: gx: 4 (over y), gy: 4 (over z_lo, core), gz: 8 (over x, z_hi).
Axes of the slice: x: 4, y: 4, z: 4 (z_hi: 2, z_lo: 2; z = z_hi * 2 + z_lo), core: 2. Of those that a mesh axis runs over, the one named last changes fastest.
Arguments:
- orbitals: float32 [16, 32, 128, 1024], P(None, 'gx', 'gy', 'gz'), may hold values from -9 to 9, as said below
- potential: float32 [32, 128, 1024], P('gx', 'gy', 'gz'), may hold values from -6 to 0
Outputs:
- filtered: float32 [16, 32, 128, 1024], P(None, 'gx', 'gy', 'gz')
- gram: float32 [16, 16], replicated
- projected: float32 [16, 16], replicated
The draws below stay inside these ranges and needn't reach their ends.
Inputs may be any that keep to these rules, and one draw needn't show every extreme that they name: `orbitals`: real entries.
All inputs are finite; a program needn't handle non-finite values.
Results may differ from the reference program's by a relative error of at most 0.000075.
Values sent between devices are 32-bit elements; how exact they have to be, the bound alone decides.
A program may use at most 128 MiB of HBM per device.

```python
import math
import jax
import jax.numpy as jnp
from jax import lax

NB = 16
NX = 32
NY = 128
NZ = 1024
NCELLS = 4194304


def plane_factors(key, count, low, high):
    return jnp.exp(jax.random.uniform(key, (count,), jnp.float32, math.log(low), math.log(high)))


def draw_orbitals(key, part):
    keys = jax.random.split(key, 7)
    low, high = (0.4, 2.0)
    along_x = plane_factors(keys[0], NX, low, high)
    along_y = plane_factors(keys[1], NY, low, high)
    along_z = plane_factors(keys[2], NZ, low, high)
    offsets = jax.random.uniform(keys[3], (NB,), jnp.float32, -1.2, 1.2)
    mixing = jax.random.normal(keys[4], (NB, 4), jnp.float32) * 0.6
    shared = jnp.clip(jax.random.normal(keys[5], (4, NX, NY, NZ), jnp.float32), -4.0, 4.0)
    own = jnp.clip(jax.random.normal(keys[6], (NB, NX, NY, NZ), jnp.float32), -4.0, 4.0)
    envelope = along_x[:, None, None] * along_y[None, :, None] * along_z[None, None, :]
    inner = offsets[:, None, None, None] + own
    for which in range(4):
        inner = inner + mixing[:, which][:, None, None, None] * shared[which][None]
    return jnp.clip(0.5 * envelope[None] * inner, -9.0, 9.0).astype(jnp.float32)


def block_scale(own_key, shape, cuts, smallest, high):
    gain, own = 1.0, jax.random.fold_in(own_key, 6)
    for position, blocks in cuts:
        steps = jnp.exp(jax.random.uniform(jax.random.fold_in(own, position), (blocks,), jnp.float32, smallest / len(cuts), high / len(cuts)))
        gain = gain * jnp.repeat(steps, shape[position] // blocks).reshape([-1 if axis == position else 1 for axis in range(len(shape))])
    return gain


def setup_inputs(seed: int = 0) -> dict:
    streams_of = jax.random.split(jax.random.key(seed), 3)
    orbitals = draw_orbitals(jax.random.fold_in(streams_of[2], 71), 0)
    potential = jnp.clip(-6.0 + 6.0 * jax.random.uniform(streams_of[1], (NX, NY, NZ), jnp.float32) ** block_scale(streams_of[1], (NX, NY, NZ), ((0, 4), (1, 4), (2, 8)), -0.2, 0.2), -6.0, 0.0)
    return dict(orbitals=orbitals, potential=potential)


coefs = (-205.0 / 72.0, 8.0 / 5.0, -1.0 / 5.0, 8.0 / 315.0, -1.0 / 560.0)
kinetic = -0.5 / 0.25
spread = 20.0
middle = 25.0
sigma_one = spread / (-6.0 - middle)
sigma_two = 1.0 / (2.0 / sigma_one - sigma_one)


def hamiltonian(field, potential):
    total = 3.0 * coefs[0] * field
    for step in range(1, 5):
        for axis in range(3):
            total = total + coefs[step] * (jnp.roll(field, -step, axis) + jnp.roll(field, step, axis))
    return kinetic * total + potential * field


def one_orbital(field, potential):
    first = (sigma_one / spread) * (hamiltonian(field, potential) - middle * field)
    second = (2.0 * sigma_two / spread) * (hamiltonian(first, potential) - middle * first) - sigma_one * sigma_two * field
    return second, hamiltonian(second, potential)


def reference(orbitals, potential):
    filtered, image = lax.map(lambda field: one_orbital(field, potential), orbitals)
    flat = filtered.reshape(NB, NCELLS)
    flat_image = image.reshape(NB, NCELLS)
    gram = jnp.dot(flat, flat.T, precision=lax.Precision.HIGHEST, preferred_element_type=jnp.float32) / NCELLS
    projected = jnp.dot(flat, flat_image.T, precision=lax.Precision.HIGHEST, preferred_element_type=jnp.float32) / NCELLS
    return filtered, gram, projected
```

```python
import functools

import jax
import jax.numpy as jnp
import ml_dtypes
import numpy as np
from jax import lax
from jax.experimental import pallas as pl
from jax.experimental.pallas import tpu as pltpu
from jax.sharding import PartitionSpec as P

MESH = pl.DeviceIdType.MESH
f32, bf16 = jnp.float32, jnp.bfloat16

coefs = (-205.0 / 72.0, 8.0 / 5.0, -1.0 / 5.0, 8.0 / 315.0, -1.0 / 560.0)
reach = 4
kinetic = -0.5 / 0.25
spread = 20.0
middle = 25.0
sigma_one = spread / (-6.0 - middle)
sigma_two = 1.0 / (2.0 / sigma_one - sigma_one)

axes = ("gx", "gy", "gz")
count, size_x, size_y, size_z = 16, 8, 32, 128
pairs = count // 2
cells = size_x * size_y
half = size_y // 2


def two_parts(matrix):
    high = matrix.astype(ml_dtypes.bfloat16)
    low = (matrix - high.astype(np.float64)).astype(ml_dtypes.bfloat16)
    return high, low


def weight(distance):
    return kinetic * coefs[abs(distance)] if 1 <= abs(distance) <= reach else 0.0


def constants():
    along_y = np.zeros((cells, cells))
    faces_y = np.zeros((cells, 2 * size_x * reach))
    for x in range(size_x):
        for y in range(size_y):
            for other in range(size_y):
                along_y[x * size_y + y, x * size_y + other] = weight(other - y)
            for r in range(reach):
                faces_y[x * size_y + y, x * reach + r] = weight(r - reach - y)
                faces_y[x * size_y + y, (size_x + x) * reach + r] = weight(size_y + r - y)
    along_z = np.zeros((size_z, size_z))
    faces_z = np.zeros((4 * reach, 2 * size_z))
    for z in range(size_z):
        for other in range(size_z):
            along_z[other, z] = weight(other - z)
        for r in range(reach):
            for o in range(2):
                faces_z[o * reach + r, o * size_z + z] = weight(r - reach - z)
                faces_z[(2 + o) * reach + r, o * size_z + z] = weight(size_z + r - z)
    pick_z = np.zeros((4 * reach, 2 * size_z))
    for r in range(reach):
        for o in range(2):
            pick_z[o * reach + r, o * size_z + r] = 1.0
            pick_z[(2 + o) * reach + r, o * size_z + size_z - reach + r] = 1.0
    gather = np.zeros((256, 128))
    for j in range(count):
        gather[8 * j : 8 * j + 8, j] = 1.0
        gather[128 + 8 * j : 128 + 8 * j + 8, count + j] = 1.0
    yh, yl = two_parts(along_y)
    fh, fl = two_parts(faces_y)
    zh, zl = two_parts(along_z)
    ch, cl = two_parts(faces_z)
    return (
        np.concatenate([yh, yh, yl], axis=1),
        np.concatenate([fh, fh, fl], axis=1),
        np.concatenate([zh, zh, zl], axis=0),
        np.concatenate([ch, ch, cl], axis=0),
        np.concatenate([pick_z, pick_z], axis=1).astype(ml_dtypes.bfloat16),
        gather.astype(ml_dtypes.bfloat16),
    )


def split(value):
    high = value.astype(bf16)
    return high, (value - high.astype(f32)).astype(bf16)


def dot(left, right, dims=((1,), (0,))):
    return lax.dot_general(left, right, (dims, ((), ())), preferred_element_type=f32)


def kernel(
    scale,
    o_ref, v_ref, ay_ref, fy_ref, az_ref, cz_ref, pick_ref, gather_ref,
    out_ref, gram_ref, proj_ref,
    first_ref, image_ref, xlo, xhi, xlo3, xhi3, ylo, yhi, ysl, ysh, zr, zs, sum_x, sum_y, sum_z,
    send_sem, recv_sem, sum_send, sum_recv,
):
    sizes = {a: lax.axis_size(a) for a in axes}
    me = {a: lax.axis_index(a) for a in axes}
    right = {a: lax.rem(me[a] + 1, sizes[a]) for a in axes}
    left = {a: lax.rem(me[a] + sizes[a] - 1, sizes[a]) for a in axes}

    barrier = pltpu.get_barrier_semaphore()
    greeted = 0
    for a in axes:
        for step in range(1, sizes[a]):
            pl.semaphore_signal(
                barrier, inc=1, device_id={a: lax.rem(me[a] + step, sizes[a])}, device_id_type=MESH
            )
            greeted += 1
    pl.semaphore_wait(barrier, greeted)

    def remote(src, dst, e, way, c, device):
        return pltpu.make_async_remote_copy(
            src_ref=src, dst_ref=dst, send_sem=send_sem.at[e, way], recv_sem=recv_sem.at[e, way, c],
            device_id=device, device_id_type=MESH,
        )

    def x_copies(e, field, two, c):
        if e < 2:
            return (
                remote(field.at[two, 0:reach], xhi.at[e, two], e, 0, c, {"gx": left["gx"]}),
                remote(field.at[two, size_x - reach : size_x], xlo.at[e, two], e, 1, c, {"gx": right["gx"]}),
            )
        return (
            remote(field.at[two, 0:reach, 0:half], xhi3.at[two], e, 0, c, {"gx": left["gx"]}),
            remote(field.at[two, size_x - reach : size_x, half:size_y], xlo3.at[two], e, 1, c, {"gx": right["gx"]}),
        )

    def yz_copies(e, two, one, c):
        low, high = pl.ds(0, 2 * reach), pl.ds(2 * reach, 2 * reach)
        return (
            remote(ysl.at[e, two], yhi.at[e, two], e, 2, c, {"gy": left["gy"]}),
            remote(ysh.at[e, two], ylo.at[e, two], e, 3, c, {"gy": right["gy"]}),
            remote(zs.at[e, one, low], zr.at[e, one, high], e, 4, c, {"gz": left["gz"]}),
            remote(zs.at[e, one, high], zr.at[e, one, low], e, 5, c, {"gz": right["gz"]}),
        )

    def pair(c):
        return pl.ds(2 * c, 2)

    def rows(ref, o):
        return ref[o].reshape(cells, size_z)

    def pack_send(e, field, c):
        for i in range(2):
            o = 2 * c + i
            for x in range(size_x):
                ysl[e, o, x * reach : (x + 1) * reach, :] = field[o, x, 0:reach, :]
                ysh[e, o, x * reach : (x + 1) * reach, :] = field[o, x, size_y - reach : size_y, :]
        h0, l0 = split(rows(field, 2 * c))
        h1, l1 = split(rows(field, 2 * c + 1))
        zs[e, c] = dot(pick_ref[...], jnp.concatenate([h0, h1, l0, l1], axis=1), ((1,), (1,)))
        for copy in yz_copies(e, pair(c), c, c):
            copy.start()

    def inner_yz(field, c):
        h0, l0 = split(rows(field, 2 * c))
        h1, l1 = split(rows(field, 2 * c + 1))
        high, low = jnp.concatenate([h0, h1], axis=1), jnp.concatenate([l0, l1], axis=1)
        y_part = dot(ay_ref[...], jnp.concatenate([high, low, high], axis=0))
        z_part = dot(
            jnp.concatenate(
                [jnp.concatenate([h0, l0, h0], axis=1), jnp.concatenate([h1, l1, h1], axis=1)], axis=0
            ),
            az_ref[...],
        )
        return y_part, z_part

    def faces_yz(e, c):
        around = jnp.concatenate(
            [jnp.concatenate([ylo[e, 2 * c + i], yhi[e, 2 * c + i]], axis=0) for i in range(2)], axis=1
        )
        high, low = split(around)
        y_part = dot(fy_ref[...], jnp.concatenate([high, low, high], axis=0))
        around = zr[e, c]
        high = around.astype(bf16).astype(f32)
        turned = jnp.concatenate([high, around - high, high], axis=0).T.astype(bf16)
        return y_part + dot(turned, cz_ref[...])

    def along_x(get, x):
        total = None
        for k in range(1, reach + 1):
            near = [v for v in (get(x - k), get(x + k)) if v is not None]
            if near:
                term = (near[0] if len(near) == 1 else near[0] + near[1]) * weight(k)
                total = term if total is None else total + term
        return total

    def hamiltonian(e, field, c, shift, write):
        y_part, z_part = inner_yz(field, c)
        around = None if e is None else faces_yz(e, c)
        for i in range(2):
            o = 2 * c + i

            def get(x):
                if x < 0:
                    return None if e is None else xlo[e, o, reach + x]
                if x >= size_x:
                    return None if e is None else xhi[e, o, x - size_x]
                return field[o, x]

            for x in range(size_x):
                block = slice(x * size_y, (x + 1) * size_y)
                lanes = slice(i * size_z, (i + 1) * size_z)
                value = y_part[block, lanes] + z_part[i * cells + x * size_y : i * cells + (x + 1) * size_y]
                if around is not None:
                    value = value + around[block, lanes]
                value = value + along_x(get, x)
                value = value + (v_ref[x] + (3.0 * kinetic * coefs[0] - shift)) * field[o, x]
                write(o, x, value)

    def wait_all(e, field, c):
        for copy in x_copies(e, field, pair(c), c) + yz_copies(e, pair(c), c, c):
            copy.wait_recv()

    def each(body):
        lax.fori_loop(0, pairs, lambda c, carry: (body(c), carry)[1], 0)

    def start_first(c):
        for copy in x_copies(0, o_ref, pair(c), c):
            copy.start()

    each(start_first)
    each(functools.partial(pack_send, 0, o_ref))

    def step_one(c):
        wait_all(0, o_ref, c)

        def write(o, x, value):
            first_ref[o, x] = value * (sigma_one / spread)

        hamiltonian(0, o_ref, c, middle, write)
        for copy in x_copies(1, first_ref, pair(c), c):
            copy.start()
        pack_send(1, first_ref, c)

    each(step_one)

    def step_two(c):
        wait_all(1, first_ref, c)

        def write(o, x, value):
            out_ref[o, x] = value * (2.0 * sigma_two / spread) - (sigma_one * sigma_two) * o_ref[o, x]

        hamiltonian(1, first_ref, c, middle, write)
        for copy in x_copies(2, out_ref, pair(c), c):
            copy.start()
        pack_send(2, out_ref, c)

        def write_image(o, x, value):
            image_ref[o, x] = value

        hamiltonian(None, out_ref, c, 0.0, write_image)

    each(step_two)

    def block(ref, x, tile):
        return split(ref[:, x, tile * 8 : (tile + 1) * 8, :].reshape(8 * count, size_z))

    def inner_block(x, tiles, with_gram):
        left, right = [], []
        for tile in tiles:
            fh, fl = block(out_ref, x, tile)
            gh, gl = block(image_ref, x, tile)
            left.append(jnp.concatenate([fh, fh, fl], axis=1))
            other = jnp.concatenate([gh, gl, gh], axis=1)
            if with_gram:
                other = jnp.concatenate([jnp.concatenate([fh, fl, fh], axis=1), other], axis=0)
            right.append(other)
        return dot(jnp.concatenate(left, axis=1), jnp.concatenate(right, axis=1), ((1,), (1,)))

    def with_gram(x, total):
        return total + inner_block(x, (0, 1), True) + inner_block(x, (2, 3), True)

    inner = lax.fori_loop(0, size_x, with_gram, jnp.zeros((8 * count, 16 * count), f32))

    def step_three(c):
        wait_all(2, out_ref, c)
        around = faces_yz(2, c)
        for i in range(2):
            o = 2 * c + i
            for x in range(size_x):
                value = around[x * size_y : (x + 1) * size_y, i * size_z : (i + 1) * size_z]
                if x < reach:
                    cross = along_x(lambda p: xlo3[o, reach + p] if p < 0 else None, x)
                    image_ref[o, x, 0:half] = value[0:half]
                    image_ref[o, x, half:size_y] = value[half:size_y] + 2.0 * cross
                else:
                    cross = along_x(lambda p: xhi3[o, p - size_x] if p >= size_x else None, x)
                    image_ref[o, x, 0:half] = value[0:half] + 2.0 * cross
                    image_ref[o, x, half:size_y] = value[half:size_y]

    each(step_three)

    def without_gram(x, total):
        return total + inner_block(x, (0, 1), False) + inner_block(x, (2, 3), False)

    outer = lax.fori_loop(0, size_x, without_gram, jnp.zeros((8 * count, 8 * count), f32))
    total = jnp.concatenate([inner[:, : 8 * count], inner[:, 8 * count :] + outer], axis=1)
    row = lax.broadcasted_iota(jnp.int32, total.shape, 0)
    lane = lax.broadcasted_iota(jnp.int32, total.shape, 1)
    total = jnp.where((row & 7) == (lane & 7), total, 0.0)
    total = total.reshape(count, 8, 16 * count).sum(axis=1)
    high, low = split(total)
    rest = (total - high.astype(f32) - low.astype(f32)).astype(bf16)
    share = dot(high, gather_ref[...]) + dot(low, gather_ref[...]) + dot(rest, gather_ref[...])

    for position, (a, slots) in enumerate(zip(axes, (sum_x, sum_y, sum_z))):
        slots[me[a]] = share

        def sum_copy(step):
            return pltpu.make_async_remote_copy(
                src_ref=slots.at[me[a]], dst_ref=slots.at[me[a]],
                send_sem=sum_send.at[position, step - 1], recv_sem=sum_recv.at[position, step - 1],
                device_id={a: lax.rem(me[a] + step, sizes[a])}, device_id_type=MESH,
            )

        copies = [sum_copy(step) for step in range(1, sizes[a])]
        for copy in copies:
            copy.start()
        for copy in copies:
            copy.wait()
        share = slots[0]
        for other in range(1, sizes[a]):
            share = share + slots[other]

    share = share * scale
    turned = share.T
    gram_ref[...] = share[:, 0:count]
    proj_ref[...] = 0.5 * (share[:, count : 2 * count] + turned[count : 2 * count, :])

    everything = pl.ds(0, count)
    for e, field in enumerate((o_ref, first_ref, out_ref)):
        for copy in x_copies(e, field, everything, 0) + yz_copies(e, everything, pl.ds(0, pairs), 0):
            copy.wait_send()


def shards(orbitals, potential):
    sizes = [lax.axis_size(a) for a in axes]
    total = cells * size_z * sizes[0] * sizes[1] * sizes[2]
    whole = pl.BlockSpec(memory_space=pltpu.VMEM)
    vmem = lambda *shape: pltpu.VMEM(shape, f32)
    return pl.pallas_call(
        functools.partial(kernel, 1.0 / total),
        out_shape=(
            jax.ShapeDtypeStruct(orbitals.shape, f32),
            jax.ShapeDtypeStruct((count, count), f32),
            jax.ShapeDtypeStruct((count, count), f32),
        ),
        in_specs=[whole] * 8,
        out_specs=(whole, whole, whole),
        scratch_shapes=[
            vmem(count, size_x, size_y, size_z),
            vmem(count, size_x, size_y, size_z),
            vmem(2, count, reach, size_y, size_z),
            vmem(2, count, reach, size_y, size_z),
            vmem(count, reach, half, size_z),
            vmem(count, reach, half, size_z),
            vmem(3, count, size_x * reach, size_z),
            vmem(3, count, size_x * reach, size_z),
            vmem(3, count, size_x * reach, size_z),
            vmem(3, count, size_x * reach, size_z),
            vmem(3, pairs, 4 * reach, cells),
            vmem(3, pairs, 4 * reach, cells),
            vmem(sizes[0], count, 128),
            vmem(sizes[1], count, 128),
            vmem(sizes[2], count, 128),
            pltpu.SemaphoreType.DMA((3, 6)),
            pltpu.SemaphoreType.DMA((3, 6, pairs)),
            pltpu.SemaphoreType.DMA((3, max(sizes))),
            pltpu.SemaphoreType.DMA((3, max(sizes))),
        ],
        compiler_params=pltpu.CompilerParams(
            collective_id=0, has_side_effects=True, vmem_limit_bytes=56 << 20
        ),
    )(orbitals, potential, *(jnp.asarray(c) for c in constants()))


def solution(mesh):
    placed = (P(None, "gx", "gy", "gz"), P("gx", "gy", "gz"))
    return jax.shard_map(
        shards,
        mesh=mesh,
        in_specs=placed,
        out_specs=(P(None, "gx", "gy", "gz"), P(), P()),
        check_vma=False,
    )
```

```python
import functools

import jax
import jax.numpy as jnp
import ml_dtypes
import numpy as np
from jax import lax
from jax.experimental import pallas as pl
from jax.experimental.pallas import tpu as pltpu
from jax.sharding import PartitionSpec as P

MESH = pl.DeviceIdType.MESH
f32, bf16 = jnp.float32, jnp.bfloat16

coefs = (-205.0 / 72.0, 8.0 / 5.0, -1.0 / 5.0, 8.0 / 315.0, -1.0 / 560.0)
reach = 4
kinetic = -0.5 / 0.25
spread = 20.0
middle = 25.0
sigma_one = spread / (-6.0 - middle)
sigma_two = 1.0 / (2.0 / sigma_one - sigma_one)

axes = ("gx", "gy", "gz")
count, size_x, size_y, size_z = 16, 8, 32, 128
pairs = count // 2
cells = size_x * size_y
half = size_y // 2


def two_parts(matrix):
    high = matrix.astype(ml_dtypes.bfloat16)
    low = (matrix - high.astype(np.float64)).astype(ml_dtypes.bfloat16)
    return high, low


def weight(distance):
    return kinetic * coefs[abs(distance)] if 1 <= abs(distance) <= reach else 0.0


def constants():
    along_y = np.zeros((cells, cells))
    faces_y = np.zeros((cells, 2 * size_x * reach))
    for x in range(size_x):
        for y in range(size_y):
            for other in range(size_y):
                along_y[x * size_y + y, x * size_y + other] = weight(other - y)
            for r in range(reach):
                faces_y[x * size_y + y, x * reach + r] = weight(r - reach - y)
                faces_y[x * size_y + y, (size_x + x) * reach + r] = weight(size_y + r - y)
    along_z = np.zeros((size_z, size_z))
    faces_z = np.zeros((4 * reach, 2 * size_z))
    for z in range(size_z):
        for other in range(size_z):
            along_z[other, z] = weight(other - z)
        for r in range(reach):
            for o in range(2):
                faces_z[o * reach + r, o * size_z + z] = weight(r - reach - z)
                faces_z[(2 + o) * reach + r, o * size_z + z] = weight(size_z + r - z)
    pick_z = np.zeros((4 * reach, 2 * size_z))
    for r in range(reach):
        for o in range(2):
            pick_z[o * reach + r, o * size_z + r] = 1.0
            pick_z[(2 + o) * reach + r, o * size_z + size_z - reach + r] = 1.0
    gather = np.zeros((256, 128))
    for j in range(count):
        gather[8 * j : 8 * j + 8, j] = 1.0
        gather[128 + 8 * j : 128 + 8 * j + 8, count + j] = 1.0
    yh, yl = two_parts(along_y)
    fh, fl = two_parts(faces_y)
    zh, zl = two_parts(along_z)
    ch, cl = two_parts(faces_z)
    return (
        np.concatenate([yh, yh, yl], axis=1),
        np.concatenate([fh, fh, fl], axis=1),
        np.concatenate([zh, zh, zl], axis=0),
        np.concatenate([ch, ch, cl], axis=0),
        np.concatenate([pick_z, pick_z], axis=1).astype(ml_dtypes.bfloat16),
        gather.astype(ml_dtypes.bfloat16),
    )


def split(value):
    high = value.astype(bf16)
    return high, (value - high.astype(f32)).astype(bf16)


def dot(left, right, dims=((1,), (0,))):
    return lax.dot_general(left, right, (dims, ((), ())), preferred_element_type=f32)


def kernel(
    scale,
    o_hbm, v_hbm, ay_hbm, fy_hbm, az_hbm, cz_hbm, pick_hbm, gather_hbm,
    out_ref, gram_ref, proj_ref,
    o_ref, v_ref, ay_ref, fy_ref, az_ref, cz_ref, pick_ref, gather_ref,
    first_ref, image_ref, cross_ref, xlo, xhi, xlo3, xhi3, ylo, yhi, ysl, ysh, zr, zs, sum_one, sum_two,
    load_sem, send_sem, recv_sem, sum_send, sum_recv,
):
    loads = [
        pltpu.make_async_copy(src, dst, load_sem.at[i])
        for i, (src, dst) in enumerate((
            (o_hbm, o_ref), (pick_hbm, pick_ref), (v_hbm, v_ref), (ay_hbm, ay_ref), (fy_hbm, fy_ref),
            (az_hbm, az_ref), (cz_hbm, cz_ref), (gather_hbm, gather_ref),
        ))
    ]
    for load in loads:
        load.start()
    sizes = {a: lax.axis_size(a) for a in axes}
    me = {a: lax.axis_index(a) for a in axes}
    right = {a: lax.rem(me[a] + 1, sizes[a]) for a in axes}
    left = {a: lax.rem(me[a] + sizes[a] - 1, sizes[a]) for a in axes}

    def device(x, y, z):
        return (x * sizes["gy"] + y) * sizes["gz"] + z

    inner_z, outer_z = lax.rem(me["gz"], 2), me["gz"] // 2
    outer_size = sizes["gz"] // 2
    near = [
        device(me["gx"], lax.rem(me["gy"] + y, sizes["gy"]), outer_z * 2 + lax.rem(inner_z + z, 2))
        for y in range(sizes["gy"]) for z in range(2) if y + z
    ]
    far = [
        device(lax.rem(me["gx"] + x, sizes["gx"]), me["gy"], lax.rem(outer_z + z, outer_size) * 2 + inner_z)
        for x in range(sizes["gx"]) for z in range(outer_size) if x + z
    ]
    beside = device(me["gx"], me["gy"], lax.rem(me["gz"] + sizes["gz"] + 2 * inner_z - 1, sizes["gz"]))

    barrier = pltpu.get_barrier_semaphore()
    greeted = near + far + [beside]
    for other in greeted:
        pl.semaphore_signal(barrier, inc=1, device_id=other, device_id_type=pl.DeviceIdType.LOGICAL)
    pl.semaphore_wait(barrier, len(greeted))

    def remote(src, dst, e, way, c, device):
        return pltpu.make_async_remote_copy(
            src_ref=src, dst_ref=dst, send_sem=send_sem.at[e, way], recv_sem=recv_sem.at[e, way, c],
            device_id=device, device_id_type=MESH,
        )

    def x_copies(e, field, two, c):
        if e < 2:
            return (
                remote(field.at[two, 0:reach], xhi.at[e, two], e, 0, c, {"gx": left["gx"]}),
                remote(field.at[two, size_x - reach : size_x], xlo.at[e, two], e, 1, c, {"gx": right["gx"]}),
            )
        return (
            remote(field.at[two, 0:reach, 0:half], xhi3.at[two], e, 0, c, {"gx": left["gx"]}),
            remote(field.at[two, size_x - reach : size_x, half:size_y], xlo3.at[two], e, 1, c, {"gx": right["gx"]}),
        )

    def yz_copies(e, two, one, c):
        low, high = pl.ds(0, 2 * reach), pl.ds(2 * reach, 2 * reach)
        return (
            remote(ysl.at[e, two], yhi.at[e, two], e, 2, c, {"gy": left["gy"]}),
            remote(ysh.at[e, two], ylo.at[e, two], e, 3, c, {"gy": right["gy"]}),
            remote(zs.at[e, one, low], zr.at[e, one, high], e, 4, c, {"gz": left["gz"]}),
            remote(zs.at[e, one, high], zr.at[e, one, low], e, 5, c, {"gz": right["gz"]}),
        )

    def pair(c):
        return pl.ds(2 * c, 2)

    def rows(ref, o):
        return ref[o].reshape(cells, size_z)

    def pack_send(e, field, c):
        for i in range(2):
            o = 2 * c + i
            for x in range(size_x):
                ysl[e, o, x * reach : (x + 1) * reach, :] = field[o, x, 0:reach, :]
                ysh[e, o, x * reach : (x + 1) * reach, :] = field[o, x, size_y - reach : size_y, :]
        h0, l0 = split(rows(field, 2 * c))
        h1, l1 = split(rows(field, 2 * c + 1))
        zs[e, c] = dot(pick_ref[...], jnp.concatenate([h0, h1, l0, l1], axis=1), ((1,), (1,)))
        for copy in yz_copies(e, pair(c), c, c):
            copy.start()

    def inner_yz(field, c):
        h0, l0 = split(rows(field, 2 * c))
        h1, l1 = split(rows(field, 2 * c + 1))
        high, low = jnp.concatenate([h0, h1], axis=1), jnp.concatenate([l0, l1], axis=1)
        y_part = dot(ay_ref[...], jnp.concatenate([high, low, high], axis=0))
        z_part = dot(
            jnp.concatenate(
                [jnp.concatenate([h0, l0, h0], axis=1), jnp.concatenate([h1, l1, h1], axis=1)], axis=0
            ),
            az_ref[...],
        )
        return y_part, z_part

    def faces_yz(e, c):
        around = jnp.concatenate(
            [jnp.concatenate([ylo[e, 2 * c + i], yhi[e, 2 * c + i]], axis=0) for i in range(2)], axis=1
        )
        high, low = split(around)
        y_part = dot(fy_ref[...], jnp.concatenate([high, low, high], axis=0))
        around = zr[e, c]
        high = around.astype(bf16).astype(f32)
        turned = jnp.concatenate([high, around - high, high], axis=0).T.astype(bf16)
        return y_part + dot(turned, cz_ref[...])

    def along_x(get, x):
        total = None
        for k in range(1, reach + 1):
            near = [v for v in (get(x - k), get(x + k)) if v is not None]
            if near:
                term = (near[0] if len(near) == 1 else near[0] + near[1]) * weight(k)
                total = term if total is None else total + term
        return total

    def hamiltonian(e, field, c, shift, write):
        y_part, z_part = inner_yz(field, c)
        around = None if e is None else faces_yz(e, c)
        for i in range(2):
            o = 2 * c + i

            def get(x):
                if x < 0:
                    return None if e is None else xlo[e, o, reach + x]
                if x >= size_x:
                    return None if e is None else xhi[e, o, x - size_x]
                return field[o, x]

            for x in range(size_x):
                block = slice(x * size_y, (x + 1) * size_y)
                lanes = slice(i * size_z, (i + 1) * size_z)
                value = y_part[block, lanes] + z_part[i * cells + x * size_y : i * cells + (x + 1) * size_y]
                if around is not None:
                    value = value + around[block, lanes]
                value = value + along_x(get, x)
                value = value + (v_ref[x] + (3.0 * kinetic * coefs[0] - shift)) * field[o, x]
                write(o, x, value)

    def wait_x(e, field, c):
        for copy in x_copies(e, field, pair(c), c):
            copy.wait_recv()

    def wait_yz(e, c):
        for copy in yz_copies(e, pair(c), c, c):
            copy.wait_recv()

    def each(body):
        lax.fori_loop(0, pairs, lambda c, carry: (body(c), carry)[1], 0)

    def start_first(c):
        for copy in x_copies(0, o_hbm, pair(c), c):
            copy.start()

    each(start_first)
    for load in loads[:2]:
        load.wait()
    each(functools.partial(pack_send, 0, o_ref))
    for load in loads[2:]:
        load.wait()

    def step_one(c):
        wait_yz(0, c)
        wait_x(0, o_hbm, c)

        def write(o, x, value):
            first_ref[o, x] = value * (sigma_one / spread)

        hamiltonian(0, o_ref, c, middle, write)
        for copy in x_copies(1, first_ref, pair(c), c):
            copy.start()
        pack_send(1, first_ref, c)

    each(step_one)

    def step_two(c):
        wait_yz(1, c)
        wait_x(1, first_ref, c)

        def write(o, x, value):
            out_ref[o, x] = value * (2.0 * sigma_two / spread) - (sigma_one * sigma_two) * o_ref[o, x]

        hamiltonian(1, first_ref, c, middle, write)
        for copy in x_copies(2, out_ref, pair(c), c):
            copy.start()
        pack_send(2, out_ref, c)

        def write_image(o, x, value):
            image_ref[o, x] = value

        hamiltonian(None, out_ref, c, 0.0, write_image)

    each(step_two)

    def add_faces(c):
        wait_yz(2, c)
        around = faces_yz(2, c)
        for i in range(2):
            o = 2 * c + i
            for x in range(size_x):
                image_ref[o, x] += around[x * size_y : (x + 1) * size_y, i * size_z : (i + 1) * size_z]

    each(add_faces)

    def block(ref, which, x, tile):
        rows = ref[which, x, tile * 8 : (tile + 1) * 8, :]
        return split(rows.reshape(8 * rows.shape[0], size_z))

    everything = slice(0, count)

    def left_parts(x, tile):
        high, low = block(out_ref, everything, x, tile)
        return jnp.concatenate([high, high, low], axis=1), jnp.concatenate([high, low, high], axis=1)

    def right_parts(ref, which, x, tile):
        high, low = block(ref, which, x, tile)
        return jnp.concatenate([high, low, high], axis=1)

    def rows_dot(left, right):
        return dot(jnp.concatenate(left, axis=1), jnp.concatenate(right, axis=1), ((1,), (1,)))

    def inner_block(x, total):
        for tiles in ((0, 1), (2, 3)):
            left, right = [], []
            for tile in tiles:
                one, other = left_parts(x, tile)
                left.append(one)
                right.append(jnp.concatenate([other, right_parts(image_ref, everything, x, tile)], axis=0))
            total = total + rows_dot(left, right)
        return total

    def collect(total, offset):
        row = lax.broadcasted_iota(jnp.int32, total.shape, 0)
        lane = lax.broadcasted_iota(jnp.int32, total.shape, 1)
        total = jnp.where((row & 7) == (lane & 7), total, 0.0)
        total = total.reshape(count, 8, total.shape[1]).sum(axis=1)
        high, low = split(total)
        rest = (total - high.astype(f32) - low.astype(f32)).astype(bf16)
        picked = dot(jnp.concatenate([high, low, rest], axis=0), gather_ref[offset : offset + total.shape[1], :])
        return picked[0:count] + picked[count : 2 * count] + picked[2 * count :]

    inner = lax.fori_loop(0, size_x, inner_block, jnp.zeros((8 * count, 16 * count), f32))
    share = collect(inner, 0)

    def add_cross(c):
        wait_x(2, out_ref, c)
        for i in range(2):
            o = 2 * c + i
            for x in range(reach):
                cross_ref[o, x, 0:half] = 2.0 * along_x(
                    lambda p: xhi3[o, p - size_x] if p >= size_x else None, size_x - reach + x
                )
                cross_ref[o, x, half:size_y] = 2.0 * along_x(lambda p: xlo3[o, reach + p] if p < 0 else None, x)

    part = count // 2
    for begin in range(0, count, part):
        lax.fori_loop(begin // 2, (begin + part) // 2, lambda c, carry: (add_cross(c), carry)[1], 0)

        def cross_block(x, total):
            for tiles, layer in (((0, 1), x + size_x - reach), ((2, 3), x)):
                left = [left_parts(layer, tile)[0] for tile in tiles]
                right = [right_parts(cross_ref, slice(begin, begin + part), x, tile) for tile in tiles]
                total = total + rows_dot(left, right)
            return total

        cross = lax.fori_loop(0, reach, cross_block, jnp.zeros((8 * count, 8 * part), f32))
        share = share + collect(cross, 8 * count + 8 * begin)

    stages = (
        (near, sum_one, me["gy"] * 2 + inner_z),
        (far, sum_two, me["gx"] * outer_size + outer_z),
    )
    sent = []
    for position, (others, slots, mine) in enumerate(stages):
        slots[mine] = share

        def sum_copy(ref, other):
            return pltpu.make_async_remote_copy(
                src_ref=ref, dst_ref=ref, send_sem=sum_send.at[position], recv_sem=sum_recv.at[position],
                device_id=other, device_id_type=pl.DeviceIdType.LOGICAL,
            )

        for other in others:
            sum_copy(slots.at[mine], other).start()
        arrived = sum_copy(slots.at[pl.ds(0, len(others))], others[0])
        arrived.wait_recv()
        sent.append(arrived)
        shares = [slots[i] for i in range(len(others) + 1)]
        while len(shares) > 1:
            shares = [shares[i] + shares[i + 1] for i in range(0, len(shares), 2)]
        share = shares[0]

    share = share * scale
    turned = share.T
    gram_ref[...] = share[:, 0:count]
    proj_ref[...] = 0.5 * (share[:, count : 2 * count] + turned[count : 2 * count, :])

    whole = pl.ds(0, count)
    for e, field in enumerate((o_hbm, first_ref, out_ref)):
        for copy in x_copies(e, field, whole, 0) + yz_copies(e, whole, pl.ds(0, pairs), 0):
            copy.wait_send()
    for copy in sent:
        copy.wait_send()


def shards(orbitals, potential):
    sizes = [lax.axis_size(a) for a in axes]
    total = cells * size_z * sizes[0] * sizes[1] * sizes[2]
    whole = pl.BlockSpec(memory_space=pltpu.VMEM)
    operands = (orbitals, potential, *(jnp.asarray(c) for c in constants()))
    vmem = lambda *shape: pltpu.VMEM(shape, f32)
    return pl.pallas_call(
        functools.partial(kernel, 1.0 / total),
        out_shape=(
            vmem(*orbitals.shape),
            vmem(count, count),
            vmem(count, count),
        ),
        in_specs=[pl.BlockSpec(memory_space=pltpu.HBM)] * len(operands),
        out_specs=(whole, whole, whole),
        scratch_shapes=[
            *(pltpu.VMEM(x.shape, x.dtype) for x in operands),
            vmem(count, size_x, size_y, size_z),
            vmem(count, size_x, size_y, size_z),
            vmem(count, reach, size_y, size_z),
            vmem(2, count, reach, size_y, size_z),
            vmem(2, count, reach, size_y, size_z),
            vmem(count, reach, half, size_z),
            vmem(count, reach, half, size_z),
            vmem(3, count, size_x * reach, size_z),
            vmem(3, count, size_x * reach, size_z),
            vmem(3, count, size_x * reach, size_z),
            vmem(3, count, size_x * reach, size_z),
            vmem(3, pairs, 4 * reach, cells),
            vmem(3, pairs, 4 * reach, cells),
            vmem(sizes[1] * 2, count, 128),
            vmem(sizes[0] * sizes[2] // 2, count, 128),
            pltpu.SemaphoreType.DMA((len(operands),)),
            pltpu.SemaphoreType.DMA((3, 6)),
            pltpu.SemaphoreType.DMA((3, 6, pairs)),
            pltpu.SemaphoreType.DMA((2,)),
            pltpu.SemaphoreType.DMA((2,)),
        ],
        compiler_params=pltpu.CompilerParams(
            collective_id=0, has_side_effects=True, vmem_limit_bytes=48 << 20
        ),
    )(*(pltpu.with_memory_space_constraint(x, pltpu.HBM) for x in operands))


def solution(mesh):
    placed = (P(None, "gx", "gy", "gz"), P("gx", "gy", "gz"))
    return jax.shard_map(
        shards,
        mesh=mesh,
        in_specs=placed,
        out_specs=(P(None, "gx", "gy", "gz"), P(), P()),
        check_vma=False,
    )
```

```python
import functools

import jax
import jax.numpy as jnp
import ml_dtypes
import numpy as np
from jax import lax
from jax.experimental import pallas as pl
from jax.experimental.pallas import tpu as pltpu
from jax.sharding import PartitionSpec as P

MESH = pl.DeviceIdType.MESH
f32, bf16 = jnp.float32, jnp.bfloat16

coefs = (-205.0 / 72.0, 8.0 / 5.0, -1.0 / 5.0, 8.0 / 315.0, -1.0 / 560.0)
reach = 4
kinetic = -0.5 / 0.25
spread = 20.0
middle = 25.0
sigma_one = spread / (-6.0 - middle)
sigma_two = 1.0 / (2.0 / sigma_one - sigma_one)

axes = ("gx", "gy", "gz")
count, size_x, size_y, size_z = 16, 8, 32, 128
pairs = count // 2
cells = size_x * size_y
half = size_y // 2


def two_parts(matrix):
    high = matrix.astype(ml_dtypes.bfloat16)
    low = (matrix - high.astype(np.float64)).astype(ml_dtypes.bfloat16)
    return high, low


def weight(distance):
    return kinetic * coefs[abs(distance)] if 1 <= abs(distance) <= reach else 0.0


def constants():
    along_y = np.zeros((cells, cells))
    faces_y = np.zeros((cells, 2 * size_x * reach))
    for x in range(size_x):
        for y in range(size_y):
            for other in range(size_y):
                along_y[x * size_y + y, x * size_y + other] = weight(other - y)
            for r in range(reach):
                faces_y[x * size_y + y, x * reach + r] = weight(r - reach - y)
                faces_y[x * size_y + y, (size_x + x) * reach + r] = weight(size_y + r - y)
    along_z = np.zeros((size_z, size_z))
    faces_z = np.zeros((4 * reach, 2 * size_z))
    for z in range(size_z):
        for other in range(size_z):
            along_z[other, z] = weight(other - z)
        for r in range(reach):
            for o in range(2):
                faces_z[o * reach + r, o * size_z + z] = weight(r - reach - z)
                faces_z[(2 + o) * reach + r, o * size_z + z] = weight(size_z + r - z)
    pick_z = np.zeros((4 * reach, 2 * size_z))
    for r in range(reach):
        for o in range(2):
            pick_z[o * reach + r, o * size_z + r] = 1.0
            pick_z[(2 + o) * reach + r, o * size_z + size_z - reach + r] = 1.0
    gather = np.zeros((256, 128))
    for j in range(count):
        gather[8 * j : 8 * j + 8, j] = 1.0
        gather[128 + 8 * j : 128 + 8 * j + 8, count + j] = 1.0
    yh, yl = two_parts(along_y)
    fh, fl = two_parts(faces_y)
    zh, zl = two_parts(along_z)
    ch, cl = two_parts(faces_z)
    return (
        np.concatenate([yh, yh, yl], axis=1),
        np.concatenate([fh, fh, fl], axis=1),
        np.concatenate([zh, zh, zl], axis=0),
        np.concatenate([ch, ch, cl], axis=0),
        np.concatenate([pick_z, pick_z], axis=1).astype(ml_dtypes.bfloat16),
        gather.astype(ml_dtypes.bfloat16),
    )


def split(value):
    high = value.astype(bf16)
    return high, (value - high.astype(f32)).astype(bf16)


def dot(left, right, dims=((1,), (0,))):
    return lax.dot_general(left, right, (dims, ((), ())), preferred_element_type=f32)


def kernel(
    scale,
    o_hbm, v_hbm, ay_hbm, fy_hbm, az_hbm, cz_hbm, pick_hbm, gather_hbm,
    out_ref, sum_ref,
    o_ref, v_ref, ay_ref, fy_ref, az_ref, cz_ref, pick_ref, gather_ref,
    first_ref, image_ref, xlo, xhi, xlo3, xhi3, ylo, yhi, ysl, ysh, zr, zs, sum_one, sum_two,
    load_sem, send_sem, recv_sem, sum_send, sum_recv,
):
    loads = [
        pltpu.make_async_copy(src, dst, load_sem.at[i])
        for i, (src, dst) in enumerate((
            (o_hbm, o_ref), (pick_hbm, pick_ref), (v_hbm, v_ref), (ay_hbm, ay_ref), (fy_hbm, fy_ref),
            (az_hbm, az_ref), (cz_hbm, cz_ref), (gather_hbm, gather_ref),
        ))
    ]
    for load in loads:
        load.start()
    sizes = {a: lax.axis_size(a) for a in axes}
    me = {a: lax.axis_index(a) for a in axes}
    right = {a: lax.rem(me[a] + 1, sizes[a]) for a in axes}
    left = {a: lax.rem(me[a] + sizes[a] - 1, sizes[a]) for a in axes}

    def device(x, y, z):
        return (x * sizes["gy"] + y) * sizes["gz"] + z

    inner_z, outer_z = lax.rem(me["gz"], 2), me["gz"] // 2
    outer_size = sizes["gz"] // 2
    def hops(steps, size):
        return min(steps, size - steps)

    near = [
        device(me["gx"], lax.rem(me["gy"] + y, sizes["gy"]), outer_z * 2 + lax.rem(inner_z + z, 2))
        for z in (1, 0) for y in sorted(range(sizes["gy"]), key=lambda y: -hops(y, sizes["gy"])) if y + z
    ]
    far = [
        device(lax.rem(me["gx"] + x, sizes["gx"]), me["gy"], lax.rem(outer_z + z, outer_size) * 2 + inner_z)
        for x, z in sorted(
            ((x, z) for x in range(sizes["gx"]) for z in range(outer_size) if x + z),
            key=lambda xz: -hops(xz[0], sizes["gx"]) - hops(xz[1], outer_size),
        )
    ]
    beside = device(me["gx"], me["gy"], lax.rem(me["gz"] + sizes["gz"] + 2 * inner_z - 1, sizes["gz"]))

    barrier = pltpu.get_barrier_semaphore()
    greeted = near + far + [beside]
    for other in greeted:
        pl.semaphore_signal(barrier, inc=1, device_id=other, device_id_type=pl.DeviceIdType.LOGICAL)
    pl.semaphore_wait(barrier, len(greeted))

    def remote(src, dst, e, way, c, device):
        return pltpu.make_async_remote_copy(
            src_ref=src, dst_ref=dst, send_sem=send_sem.at[e, way], recv_sem=recv_sem.at[e, way, c],
            device_id=device, device_id_type=MESH,
        )

    def x_copies(e, field, two, c):
        if e < 2:
            return (
                remote(field.at[two, 0:reach], xhi.at[e, two], e, 0, c, {"gx": left["gx"]}),
                remote(field.at[two, size_x - reach : size_x], xlo.at[e, two], e, 1, c, {"gx": right["gx"]}),
            )
        return (
            remote(field.at[two, 0:reach, 0:half], xhi3.at[two], e, 0, c, {"gx": left["gx"]}),
            remote(field.at[two, size_x - reach : size_x, half:size_y], xlo3.at[two], e, 1, c, {"gx": right["gx"]}),
        )

    def yz_copies(e, two, one, c):
        low, high = pl.ds(0, 2 * reach), pl.ds(2 * reach, 2 * reach)
        return (
            remote(ysl.at[e, two], yhi.at[e, two], e, 2, c, {"gy": left["gy"]}),
            remote(ysh.at[e, two], ylo.at[e, two], e, 3, c, {"gy": right["gy"]}),
            remote(zs.at[e, one, low], zr.at[e, one, high], e, 4, c, {"gz": left["gz"]}),
            remote(zs.at[e, one, high], zr.at[e, one, low], e, 5, c, {"gz": right["gz"]}),
        )

    def pair(c):
        return pl.ds(2 * c, 2)

    def rows(ref, o):
        return ref[o].reshape(cells, size_z)

    def pack_send(e, field, c):
        for i in range(2):
            o = 2 * c + i
            for x in range(size_x):
                ysl[e, o, x * reach : (x + 1) * reach, :] = field[o, x, 0:reach, :]
                ysh[e, o, x * reach : (x + 1) * reach, :] = field[o, x, size_y - reach : size_y, :]
        h0, l0 = split(rows(field, 2 * c))
        h1, l1 = split(rows(field, 2 * c + 1))
        zs[e, c] = dot(pick_ref[...], jnp.concatenate([h0, h1, l0, l1], axis=1), ((1,), (1,)))
        for copy in yz_copies(e, pair(c), c, c):
            copy.start()

    def inner_yz(field, c):
        h0, l0 = split(rows(field, 2 * c))
        h1, l1 = split(rows(field, 2 * c + 1))
        high, low = jnp.concatenate([h0, h1], axis=1), jnp.concatenate([l0, l1], axis=1)
        y_part = dot(ay_ref[...], jnp.concatenate([high, low, high], axis=0))
        z_part = dot(
            jnp.concatenate(
                [jnp.concatenate([h0, l0, h0], axis=1), jnp.concatenate([h1, l1, h1], axis=1)], axis=0
            ),
            az_ref[...],
        )
        return y_part, z_part

    def faces_yz(e, c):
        around = jnp.concatenate(
            [jnp.concatenate([ylo[e, 2 * c + i], yhi[e, 2 * c + i]], axis=0) for i in range(2)], axis=1
        )
        high, low = split(around)
        y_part = dot(fy_ref[...], jnp.concatenate([high, low, high], axis=0))
        around = zr[e, c]
        high = around.astype(bf16).astype(f32)
        turned = jnp.concatenate([high, around - high, high], axis=0).T.astype(bf16)
        return y_part + dot(turned, cz_ref[...])

    def along_x(get, x):
        total = None
        for k in range(1, reach + 1):
            near = [v for v in (get(x - k), get(x + k)) if v is not None]
            if near:
                term = (near[0] if len(near) == 1 else near[0] + near[1]) * weight(k)
                total = term if total is None else total + term
        return total

    def hamiltonian(e, field, c, shift, write):
        y_part, z_part = inner_yz(field, c)
        around = None if e is None else faces_yz(e, c)
        for i in range(2):
            o = 2 * c + i

            def get(x):
                if x < 0:
                    return None if e is None else xlo[e, o, reach + x]
                if x >= size_x:
                    return None if e is None else xhi[e, o, x - size_x]
                return field[o, x]

            for x in range(size_x):
                block = slice(x * size_y, (x + 1) * size_y)
                lanes = slice(i * size_z, (i + 1) * size_z)
                value = y_part[block, lanes] + z_part[i * cells + x * size_y : i * cells + (x + 1) * size_y]
                if around is not None:
                    value = value + around[block, lanes]
                value = value + along_x(get, x)
                value = value + (v_ref[x] + (3.0 * kinetic * coefs[0] - shift)) * field[o, x]
                write(o, x, value)

    def wait_x(e, field, c):
        for copy in x_copies(e, field, pair(c), c):
            copy.wait_recv()

    def wait_yz(e, c):
        for copy in yz_copies(e, pair(c), c, c):
            copy.wait_recv()

    def each(body):
        lax.fori_loop(0, pairs, lambda c, carry: (body(c), carry)[1], 0)

    def start_first(c):
        for copy in x_copies(0, o_hbm, pair(c), c):
            copy.start()

    each(start_first)
    for load in loads[:2]:
        load.wait()
    each(functools.partial(pack_send, 0, o_ref))
    for load in loads[2:]:
        load.wait()

    def step_one(c):
        wait_yz(0, c)
        wait_x(0, o_hbm, c)

        def write(o, x, value):
            first_ref[o, x] = value * (sigma_one / spread)

        hamiltonian(0, o_ref, c, middle, write)
        for copy in x_copies(1, first_ref, pair(c), c):
            copy.start()
        pack_send(1, first_ref, c)

    each(step_one)

    def step_two(c):
        wait_yz(1, c)
        wait_x(1, first_ref, c)

        def write(o, x, value):
            out_ref[o, x] = value * (2.0 * sigma_two / spread) - (sigma_one * sigma_two) * o_ref[o, x]

        hamiltonian(1, first_ref, c, middle, write)
        for copy in x_copies(2, out_ref, pair(c), c):
            copy.start()
        pack_send(2, out_ref, c)

        def write_image(o, x, value):
            image_ref[o, x] = value

        hamiltonian(None, out_ref, c, 0.0, write_image)

    def add_faces(c):
        wait_yz(2, c)
        around = faces_yz(2, c)
        for i in range(2):
            o = 2 * c + i
            for x in range(size_x):
                image_ref[o, x] += around[x * size_y : (x + 1) * size_y, i * size_z : (i + 1) * size_z]

    def step_two_and_faces(c):
        step_two(c)
        add_faces(c - 1)

    step_two(0)
    lax.fori_loop(1, pairs, lambda c, carry: (step_two_and_faces(c), carry)[1], 0)
    add_faces(pairs - 1)

    def block(ref, x, tile):
        return split(ref[:, x, tile * 8 : (tile + 1) * 8, :].reshape(8 * count, size_z))

    def rows_dot(left, right):
        return dot(jnp.concatenate(left, axis=1), jnp.concatenate(right, axis=1), ((1,), (1,)))

    def inner_block(x, total):
        for tiles in ((0, 1), (2, 3)):
            left, right = [], []
            for tile in tiles:
                high, low = block(out_ref, x, tile)
                other_high, other_low = block(image_ref, x, tile)
                left.append(jnp.concatenate([high, high, low], axis=1))
                right.append(
                    jnp.concatenate(
                        [
                            jnp.concatenate([high, low, high], axis=1),
                            jnp.concatenate([other_high, other_low, other_high], axis=1),
                        ],
                        axis=0,
                    )
                )
            total = total + rows_dot(left, right)
        return total

    def three_parts(value):
        high, low = split(value)
        rest = (value - high.astype(f32) - low.astype(f32)).astype(bf16)
        return jnp.concatenate([high, low, rest], axis=0)

    def added_up(parts, length):
        return parts[0:length] + parts[length : 2 * length] + parts[2 * length :]

    def collect(total):
        row = lax.broadcasted_iota(jnp.int32, total.shape, 0)
        lane = lax.broadcasted_iota(jnp.int32, total.shape, 1)
        total = jnp.where((row & 7) == (lane & 7), total, 0.0)
        total = total.reshape(count, 8, total.shape[1]).sum(axis=1)
        return added_up(dot(three_parts(total), gather_ref[...]), count)

    inner = lax.fori_loop(0, size_x, inner_block, jnp.zeros((8 * count, 16 * count), f32))
    share = collect(inner)

    def add_cross(c, share):
        wait_x(2, out_ref, c)
        sums = [[None, None] for _ in range(count)]
        for x in range(reach):
            from_high = [
                along_x(lambda p: xhi3[2 * c + j, p - size_x] if p >= size_x else None, size_x - reach + x)
                for j in range(2)
            ]
            from_low = [along_x(lambda p: xlo3[2 * c + j, reach + p] if p < 0 else None, x) for j in range(2)]
            for near, layer, begin in ((from_high, size_x - reach + x, 0), (from_low, x, half)):
                for tile in range(0, half, 8):
                    for i in range(count):
                        mine = out_ref[i, layer, begin + tile : begin + tile + 8, :]
                        for j in range(2):
                            term = mine * near[j][tile : tile + 8]
                            sums[i][j] = term if sums[i][j] is None else sums[i][j] + term
        rows = jnp.concatenate(
            [jnp.concatenate([sums[i][j][None] for i in range(count)], axis=0).sum(axis=1) for j in range(2)], axis=0
        )
        rows = added_up(dot(three_parts(rows), jnp.ones((size_z, 128), bf16)), 2 * count)
        lane = lax.broadcasted_iota(jnp.int32, (count, 128), 1)
        for j in range(2):
            share = share + jnp.where(lane == count + 2 * c + j, 2.0 * rows[j * count : (j + 1) * count], 0.0)
        return share

    share = lax.fori_loop(0, pairs, add_cross, share)
    share = share[0:8] + pltpu.roll(share[8:16], 64, 1)

    stages = (
        (near, sum_one, me["gy"] * 2 + inner_z),
        (far, sum_two, me["gx"] * outer_size + outer_z),
    )
    sent = []
    for position, (others, slots, mine) in enumerate(stages):
        slots[mine] = share

        def sum_copy(ref, other):
            return pltpu.make_async_remote_copy(
                src_ref=ref, dst_ref=ref, send_sem=sum_send.at[position], recv_sem=sum_recv.at[position],
                device_id=other, device_id_type=pl.DeviceIdType.LOGICAL,
            )

        for other in others:
            sum_copy(slots.at[mine], other).start()
        arrived = sum_copy(slots.at[pl.ds(0, len(others))], others[0])
        arrived.wait_recv()
        sent.append(arrived)
        shares = [slots[i] for i in range(len(others) + 1)]
        while len(shares) > 1:
            shares = [shares[i] + shares[i + 1] for i in range(0, len(shares), 2)]
        share = shares[0]

    sum_ref[...] = share * scale

    whole = pl.ds(0, count)
    for e, field in enumerate((o_hbm, first_ref, out_ref)):
        for copy in x_copies(e, field, whole, 0) + yz_copies(e, whole, pl.ds(0, pairs), 0):
            copy.wait_send()
    for copy in sent:
        copy.wait_send()


def finish(out_ref, sum_ref, out_hbm, gram_hbm, proj_hbm, gram_ref, proj_ref, sems):
    move = pltpu.make_async_copy(out_ref, out_hbm, sems.at[0])
    move.start()
    total = jnp.concatenate([sum_ref[...], pltpu.roll(sum_ref[...], 64, 1)], axis=0)
    turned = total.T
    gram_ref[...] = total[:, 0:count]
    proj_ref[...] = 0.5 * (total[:, count : 2 * count] + turned[count : 2 * count, :])
    moves = [
        move,
        pltpu.make_async_copy(gram_ref, gram_hbm, sems.at[1]),
        pltpu.make_async_copy(proj_ref, proj_hbm, sems.at[2]),
    ]
    for later in moves[1:]:
        later.start()
    for each in moves:
        each.wait()


def shards(orbitals, potential):
    sizes = [lax.axis_size(a) for a in axes]
    total = cells * size_z * sizes[0] * sizes[1] * sizes[2]
    operands = (orbitals, potential, *(jnp.asarray(c) for c in constants()))
    vmem = lambda *shape: pltpu.VMEM(shape, f32)
    whole, anywhere = pl.BlockSpec(memory_space=pltpu.VMEM), pl.BlockSpec(memory_space=pltpu.HBM)
    filtered, sums = pl.pallas_call(
        functools.partial(kernel, 1.0 / total),
        out_shape=(vmem(*orbitals.shape), vmem(8, 128)),
        in_specs=[anywhere] * len(operands),
        out_specs=(whole, whole),
        scratch_shapes=[
            *(pltpu.VMEM(x.shape, x.dtype) for x in operands),
            vmem(count, size_x, size_y, size_z),
            vmem(count, size_x, size_y, size_z),
            vmem(2, count, reach, size_y, size_z),
            vmem(2, count, reach, size_y, size_z),
            vmem(count, reach, half, size_z),
            vmem(count, reach, half, size_z),
            vmem(3, count, size_x * reach, size_z),
            vmem(3, count, size_x * reach, size_z),
            vmem(3, count, size_x * reach, size_z),
            vmem(3, count, size_x * reach, size_z),
            vmem(3, pairs, 4 * reach, cells),
            vmem(3, pairs, 4 * reach, cells),
            vmem(sizes[1] * 2, 8, 128),
            vmem(sizes[0] * sizes[2] // 2, 8, 128),
            pltpu.SemaphoreType.DMA((len(operands),)),
            pltpu.SemaphoreType.DMA((3, 6)),
            pltpu.SemaphoreType.DMA((3, 6, pairs)),
            pltpu.SemaphoreType.DMA((2,)),
            pltpu.SemaphoreType.DMA((2,)),
        ],
        compiler_params=pltpu.CompilerParams(
            collective_id=0, has_side_effects=True, vmem_limit_bytes=48 << 20
        ),
    )(*(pltpu.with_memory_space_constraint(x, pltpu.HBM) for x in operands))
    return pl.pallas_call(
        finish,
        out_shape=(
            jax.ShapeDtypeStruct(orbitals.shape, f32),
            jax.ShapeDtypeStruct((count, count), f32),
            jax.ShapeDtypeStruct((count, count), f32),
        ),
        in_specs=[whole, whole],
        out_specs=(anywhere, anywhere, anywhere),
        scratch_shapes=[vmem(count, count), vmem(count, count), pltpu.SemaphoreType.DMA((3,))],
        compiler_params=pltpu.CompilerParams(vmem_limit_bytes=8 << 20),
    )(pltpu.with_memory_space_constraint(filtered, pltpu.VMEM), pltpu.with_memory_space_constraint(sums, pltpu.VMEM))


def solution(mesh):
    placed = (P(None, "gx", "gy", "gz"), P("gx", "gy", "gz"))
    return jax.shard_map(
        shards,
        mesh=mesh,
        in_specs=placed,
        out_specs=(P(None, "gx", "gy", "gz"), P(), P()),
        check_vma=False,
    )
```

```python
import functools

import jax
import jax.numpy as jnp
import ml_dtypes
import numpy as np
from jax import lax
from jax.experimental import pallas as pl
from jax.experimental.pallas import tpu as pltpu
from jax.sharding import PartitionSpec as P

MESH = pl.DeviceIdType.MESH
f32, bf16 = jnp.float32, jnp.bfloat16

coefs = (-205.0 / 72.0, 8.0 / 5.0, -1.0 / 5.0, 8.0 / 315.0, -1.0 / 560.0)
reach = 4
kinetic = -0.5 / 0.25
spread = 20.0
middle = 25.0
sigma_one = spread / (-6.0 - middle)
sigma_two = 1.0 / (2.0 / sigma_one - sigma_one)

axes = ("gx", "gy", "gz")
count, size_x, size_y, size_z = 16, 8, 32, 128
pairs = count // 2
cells = size_x * size_y
half = size_y // 2


def two_parts(matrix):
    high = matrix.astype(ml_dtypes.bfloat16)
    low = (matrix - high.astype(np.float64)).astype(ml_dtypes.bfloat16)
    return high, low


def weight(distance):
    return kinetic * coefs[abs(distance)] if 1 <= abs(distance) <= reach else 0.0


def constants():
    along_y = np.zeros((cells, cells))
    faces_y = np.zeros((cells, 2 * size_x * reach))
    for x in range(size_x):
        for y in range(size_y):
            for other in range(size_y):
                along_y[x * size_y + y, x * size_y + other] = weight(other - y)
            for r in range(reach):
                faces_y[x * size_y + y, x * reach + r] = weight(r - reach - y)
                faces_y[x * size_y + y, (size_x + x) * reach + r] = weight(size_y + r - y)
    along_z = np.zeros((size_z, size_z))
    faces_z = np.zeros((4 * reach, 2 * size_z))
    for z in range(size_z):
        for other in range(size_z):
            along_z[other, z] = weight(other - z)
        for r in range(reach):
            for o in range(2):
                faces_z[o * reach + r, o * size_z + z] = weight(r - reach - z)
                faces_z[(2 + o) * reach + r, o * size_z + z] = weight(size_z + r - z)
    pick_z = np.zeros((4 * reach, 2 * size_z))
    for r in range(reach):
        for o in range(2):
            pick_z[o * reach + r, o * size_z + r] = 1.0
            pick_z[(2 + o) * reach + r, o * size_z + size_z - reach + r] = 1.0
    gather = np.zeros((256, 128))
    for j in range(count):
        gather[8 * j : 8 * j + 8, j] = 1.0
        gather[128 + 8 * j : 128 + 8 * j + 8, count + j] = 1.0
    yh, yl = two_parts(along_y)
    fh, fl = two_parts(faces_y)
    zh, zl = two_parts(along_z)
    ch, cl = two_parts(faces_z)
    return (
        np.concatenate([yh, yh, yl], axis=1),
        np.concatenate([fh, fh, fl], axis=1),
        np.concatenate([zh, zh, zl], axis=0),
        np.concatenate([ch, ch, cl], axis=0),
        np.concatenate([pick_z, pick_z], axis=1).astype(ml_dtypes.bfloat16),
        gather.astype(ml_dtypes.bfloat16),
    )


def split(value):
    high = value.astype(bf16)
    return high, (value - high.astype(f32)).astype(bf16)


def dot(left, right, dims=((1,), (0,))):
    return lax.dot_general(left, right, (dims, ((), ())), preferred_element_type=f32)


def kernel(
    scale,
    o_hbm, v_hbm, ay_hbm, fy_hbm, az_hbm, cz_hbm, pick_hbm, gather_hbm,
    out_ref, sum_ref,
    o_ref, v_ref, ay_ref, fy_ref, az_ref, cz_ref, pick_ref, gather_ref,
    first_ref, image_ref, xlo, xhi, xlo3, xhi3, ylo, yhi, ysl, ysh, zr, zs, sum_one, sum_two,
    pair_sem, load_sem, send_sem, recv_sem, sum_send, sum_recv,
):
    def load_pair(c):
        return pltpu.make_async_copy(o_hbm.at[pl.ds(2 * c, 2)], o_ref.at[pl.ds(2 * c, 2)], pair_sem.at[c])

    for c in range(pairs):
        load_pair(c).start()

    sizes = {a: lax.axis_size(a) for a in axes}
    me = {a: lax.axis_index(a) for a in axes}
    right = {a: lax.rem(me[a] + 1, sizes[a]) for a in axes}
    left = {a: lax.rem(me[a] + sizes[a] - 1, sizes[a]) for a in axes}

    def device(x, y, z):
        return (x * sizes["gy"] + y) * sizes["gz"] + z

    inner_z, outer_z = lax.rem(me["gz"], 2), me["gz"] // 2
    outer_size = sizes["gz"] // 2
    def hops(steps, size):
        return min(steps, size - steps)

    near = [
        device(me["gx"], lax.rem(me["gy"] + y, sizes["gy"]), outer_z * 2 + lax.rem(inner_z + z, 2))
        for z in (1, 0) for y in sorted(range(sizes["gy"]), key=lambda y: -hops(y, sizes["gy"])) if y + z
    ]
    far = [
        device(lax.rem(me["gx"] + x, sizes["gx"]), me["gy"], lax.rem(outer_z + z, outer_size) * 2 + inner_z)
        for x, z in sorted(
            ((x, z) for x in range(sizes["gx"]) for z in range(outer_size) if x + z),
            key=lambda xz: -hops(xz[0], sizes["gx"]) - hops(xz[1], outer_size),
        )
    ]
    beside = device(me["gx"], me["gy"], lax.rem(me["gz"] + sizes["gz"] + 2 * inner_z - 1, sizes["gz"]))

    barrier = pltpu.get_barrier_semaphore()
    greeted = near + far + [beside]
    for other in greeted:
        pl.semaphore_signal(barrier, inc=1, device_id=other, device_id_type=pl.DeviceIdType.LOGICAL)
    pl.semaphore_wait(barrier, len(greeted))

    def remote(src, dst, e, way, c, device):
        return pltpu.make_async_remote_copy(
            src_ref=src, dst_ref=dst, send_sem=send_sem.at[e, way], recv_sem=recv_sem.at[e, way, c],
            device_id=device, device_id_type=MESH,
        )

    def x_copies(e, field, two, c):
        if e < 2:
            return (
                remote(field.at[two, 0:reach], xhi.at[e, two], e, 0, c, {"gx": left["gx"]}),
                remote(field.at[two, size_x - reach : size_x], xlo.at[e, two], e, 1, c, {"gx": right["gx"]}),
            )
        return (
            remote(field.at[two, 0:reach, 0:half], xhi3.at[two], e, 0, c, {"gx": left["gx"]}),
            remote(field.at[two, size_x - reach : size_x, half:size_y], xlo3.at[two], e, 1, c, {"gx": right["gx"]}),
        )

    def yz_copies(e, two, one, c):
        low, high = pl.ds(0, 2 * reach), pl.ds(2 * reach, 2 * reach)
        return (
            remote(ysl.at[e, two], yhi.at[e, two], e, 2, c, {"gy": left["gy"]}),
            remote(ysh.at[e, two], ylo.at[e, two], e, 3, c, {"gy": right["gy"]}),
            remote(zs.at[e, one, low], zr.at[e, one, high], e, 4, c, {"gz": left["gz"]}),
            remote(zs.at[e, one, high], zr.at[e, one, low], e, 5, c, {"gz": right["gz"]}),
        )

    def pair(c):
        return pl.ds(2 * c, 2)

    def rows(ref, o):
        return ref[o].reshape(cells, size_z)

    def pack_send(e, field, c):
        for i in range(2):
            o = 2 * c + i
            for x in range(size_x):
                ysl[e, o, x * reach : (x + 1) * reach, :] = field[o, x, 0:reach, :]
                ysh[e, o, x * reach : (x + 1) * reach, :] = field[o, x, size_y - reach : size_y, :]
        h0, l0 = split(rows(field, 2 * c))
        h1, l1 = split(rows(field, 2 * c + 1))
        zs[e, c] = dot(pick_ref[...], jnp.concatenate([h0, h1, l0, l1], axis=1), ((1,), (1,)))
        for copy in yz_copies(e, pair(c), c, c):
            copy.start()

    def inner_yz(field, c):
        h0, l0 = split(rows(field, 2 * c))
        h1, l1 = split(rows(field, 2 * c + 1))
        high, low = jnp.concatenate([h0, h1], axis=1), jnp.concatenate([l0, l1], axis=1)
        y_part = dot(ay_ref[...], jnp.concatenate([high, low, high], axis=0))
        z_part = dot(
            jnp.concatenate(
                [jnp.concatenate([h0, l0, h0], axis=1), jnp.concatenate([h1, l1, h1], axis=1)], axis=0
            ),
            az_ref[...],
        )
        return y_part, z_part

    def faces_yz(e, c):
        around = jnp.concatenate(
            [jnp.concatenate([ylo[e, 2 * c + i], yhi[e, 2 * c + i]], axis=0) for i in range(2)], axis=1
        )
        high, low = split(around)
        y_part = dot(fy_ref[...], jnp.concatenate([high, low, high], axis=0))
        around = zr[e, c]
        high = around.astype(bf16).astype(f32)
        turned = jnp.concatenate([high, around - high, high], axis=0).T.astype(bf16)
        return y_part + dot(turned, cz_ref[...])

    def along_x(get, x):
        total = None
        for k in range(1, reach + 1):
            near = [v for v in (get(x - k), get(x + k)) if v is not None]
            if near:
                term = (near[0] if len(near) == 1 else near[0] + near[1]) * weight(k)
                total = term if total is None else total + term
        return total

    def hamiltonian(e, field, c, shift, write):
        y_part, z_part = inner_yz(field, c)
        around = None if e is None else faces_yz(e, c)
        for i in range(2):
            o = 2 * c + i

            def get(x):
                if x < 0:
                    return None if e is None else xlo[e, o, reach + x]
                if x >= size_x:
                    return None if e is None else xhi[e, o, x - size_x]
                return field[o, x]

            for x in range(size_x):
                block = slice(x * size_y, (x + 1) * size_y)
                lanes = slice(i * size_z, (i + 1) * size_z)
                value = y_part[block, lanes] + z_part[i * cells + x * size_y : i * cells + (x + 1) * size_y]
                if around is not None:
                    value = value + around[block, lanes]
                value = value + along_x(get, x)
                value = value + (v_ref[x] + (3.0 * kinetic * coefs[0] - shift)) * field[o, x]
                write(o, x, value)

    def wait_x(e, field, c):
        for copy in x_copies(e, field, pair(c), c):
            copy.wait_recv()

    def wait_yz(e, c):
        for copy in yz_copies(e, pair(c), c, c):
            copy.wait_recv()

    def each(body):
        lax.fori_loop(0, pairs, lambda c, carry: (body(c), carry)[1], 0)

    def start_first(c):
        load_pair(c).wait()
        for copy in x_copies(0, o_ref, pair(c), c):
            copy.start()

    each(start_first)
    loads = [
        pltpu.make_async_copy(src, dst, load_sem.at[i])
        for i, (src, dst) in enumerate((
            (pick_hbm, pick_ref), (v_hbm, v_ref), (ay_hbm, ay_ref), (fy_hbm, fy_ref),
            (az_hbm, az_ref), (cz_hbm, cz_ref), (gather_hbm, gather_ref),
        ))
    ]
    for load in loads:
        load.start()
    loads[0].wait()
    each(functools.partial(pack_send, 0, o_ref))
    for load in loads[1:]:
        load.wait()

    def step_one(c):
        wait_yz(0, c)
        wait_x(0, o_ref, c)

        def write(o, x, value):
            first_ref[o, x] = value * (sigma_one / spread)

        hamiltonian(0, o_ref, c, middle, write)
        for copy in x_copies(1, first_ref, pair(c), c):
            copy.start()
        pack_send(1, first_ref, c)

    each(step_one)

    def step_two(c):
        wait_yz(1, c)
        wait_x(1, first_ref, c)

        def write(o, x, value):
            out_ref[o, x] = value * (2.0 * sigma_two / spread) - (sigma_one * sigma_two) * o_ref[o, x]

        hamiltonian(1, first_ref, c, middle, write)
        for copy in x_copies(2, out_ref, pair(c), c):
            copy.start()
        pack_send(2, out_ref, c)

        def write_image(o, x, value):
            image_ref[o, x] = value

        hamiltonian(None, out_ref, c, 0.0, write_image)

    def add_faces(c):
        wait_yz(2, c)
        around = faces_yz(2, c)
        for i in range(2):
            o = 2 * c + i
            for x in range(size_x):
                image_ref[o, x] += around[x * size_y : (x + 1) * size_y, i * size_z : (i + 1) * size_z]

    lag = 3

    def step_two_and_faces(c):
        step_two(c)

        @pl.when(c >= lag)
        def _():
            add_faces(c - lag)

    each(step_two_and_faces)
    lax.fori_loop(pairs - lag, pairs, lambda c, carry: (add_faces(c), carry)[1], 0)

    def block(ref, x, tile):
        return split(ref[:, x, tile * 8 : (tile + 1) * 8, :].reshape(8 * count, size_z))

    def rows_dot(left, right):
        return dot(jnp.concatenate(left, axis=1), jnp.concatenate(right, axis=1), ((1,), (1,)))

    def inner_block(x, total):
        for tiles in ((0, 1), (2, 3)):
            left, right = [], []
            for tile in tiles:
                high, low = block(out_ref, x, tile)
                other_high, other_low = block(image_ref, x, tile)
                left.append(jnp.concatenate([high, high, low], axis=1))
                right.append(
                    jnp.concatenate(
                        [
                            jnp.concatenate([high, low, high], axis=1),
                            jnp.concatenate([other_high, other_low, other_high], axis=1),
                        ],
                        axis=0,
                    )
                )
            total = total + rows_dot(left, right)
        return total

    def three_parts(value):
        high, low = split(value)
        rest = (value - high.astype(f32) - low.astype(f32)).astype(bf16)
        return jnp.concatenate([high, low, rest], axis=0)

    def added_up(parts, length):
        return parts[0:length] + parts[length : 2 * length] + parts[2 * length :]

    def collect(total):
        row = lax.broadcasted_iota(jnp.int32, total.shape, 0)
        lane = lax.broadcasted_iota(jnp.int32, total.shape, 1)
        total = jnp.where((row & 7) == (lane & 7), total, 0.0)
        total = total.reshape(count, 8, total.shape[1]).sum(axis=1)
        return added_up(dot(three_parts(total), gather_ref[...]), count)

    inner = lax.fori_loop(0, size_x, inner_block, jnp.zeros((8 * count, 16 * count), f32))
    share = collect(inner)

    def add_cross(c, share):
        wait_x(2, out_ref, c)
        sums = [[None, None] for _ in range(count)]
        for x in range(reach):
            from_high = [
                along_x(lambda p: xhi3[2 * c + j, p - size_x] if p >= size_x else None, size_x - reach + x)
                for j in range(2)
            ]
            from_low = [along_x(lambda p: xlo3[2 * c + j, reach + p] if p < 0 else None, x) for j in range(2)]
            for near, layer, begin in ((from_high, size_x - reach + x, 0), (from_low, x, half)):
                for tile in range(0, half, 8):
                    for i in range(count):
                        mine = out_ref[i, layer, begin + tile : begin + tile + 8, :]
                        for j in range(2):
                            term = mine * near[j][tile : tile + 8]
                            sums[i][j] = term if sums[i][j] is None else sums[i][j] + term
        rows = jnp.concatenate(
            [jnp.concatenate([sums[i][j][None] for i in range(count)], axis=0).sum(axis=1) for j in range(2)], axis=0
        )
        rows = added_up(dot(three_parts(rows), jnp.ones((size_z, 128), bf16)), 2 * count)
        lane = lax.broadcasted_iota(jnp.int32, (count, 128), 1)
        for j in range(2):
            share = share + jnp.where(lane == count + 2 * c + j, 2.0 * rows[j * count : (j + 1) * count], 0.0)
        return share

    share = lax.fori_loop(0, pairs, add_cross, share)
    share = share[0:8] + pltpu.roll(share[8:16], 64, 1)

    stages = (
        (near, sum_one, me["gy"] * 2 + inner_z),
        (far, sum_two, me["gx"] * outer_size + outer_z),
    )
    sent = []
    for position, (others, slots, mine) in enumerate(stages):
        slots[mine] = share

        def sum_copy(ref, other):
            return pltpu.make_async_remote_copy(
                src_ref=ref, dst_ref=ref, send_sem=sum_send.at[position], recv_sem=sum_recv.at[position],
                device_id=other, device_id_type=pl.DeviceIdType.LOGICAL,
            )

        for other in others:
            sum_copy(slots.at[mine], other).start()
        arrived = sum_copy(slots.at[pl.ds(0, len(others))], others[0])
        arrived.wait_recv()
        sent.append(arrived)
        shares = [slots[i] for i in range(len(others) + 1)]
        while len(shares) > 1:
            shares = [shares[i] + shares[i + 1] for i in range(0, len(shares), 2)]
        share = shares[0]

    sum_ref[...] = share * scale

    whole = pl.ds(0, count)
    for e, field in enumerate((o_ref, first_ref, out_ref)):
        for copy in x_copies(e, field, whole, 0) + yz_copies(e, whole, pl.ds(0, pairs), 0):
            copy.wait_send()
    for copy in sent:
        copy.wait_send()


def finish(out_ref, sum_ref, out_hbm, gram_hbm, proj_hbm, gram_ref, proj_ref, sems):
    move = pltpu.make_async_copy(out_ref, out_hbm, sems.at[0])
    move.start()
    total = jnp.concatenate([sum_ref[...], pltpu.roll(sum_ref[...], 64, 1)], axis=0)
    turned = total.T
    gram_ref[...] = total[:, 0:count]
    proj_ref[...] = 0.5 * (total[:, count : 2 * count] + turned[count : 2 * count, :])
    moves = [
        move,
        pltpu.make_async_copy(gram_ref, gram_hbm, sems.at[1]),
        pltpu.make_async_copy(proj_ref, proj_hbm, sems.at[2]),
    ]
    for later in moves[1:]:
        later.start()
    for each in moves:
        each.wait()


def shards(orbitals, potential):
    sizes = [lax.axis_size(a) for a in axes]
    total = cells * size_z * sizes[0] * sizes[1] * sizes[2]
    operands = (orbitals, potential, *(jnp.asarray(c) for c in constants()))
    vmem = lambda *shape: pltpu.VMEM(shape, f32)
    whole, anywhere = pl.BlockSpec(memory_space=pltpu.VMEM), pl.BlockSpec(memory_space=pltpu.HBM)
    filtered, sums = pl.pallas_call(
        functools.partial(kernel, 1.0 / total),
        out_shape=(vmem(*orbitals.shape), vmem(8, 128)),
        in_specs=[anywhere] * len(operands),
        out_specs=(whole, whole),
        scratch_shapes=[
            *(pltpu.VMEM(x.shape, x.dtype) for x in operands),
            vmem(count, size_x, size_y, size_z),
            vmem(count, size_x, size_y, size_z),
            vmem(2, count, reach, size_y, size_z),
            vmem(2, count, reach, size_y, size_z),
            vmem(count, reach, half, size_z),
            vmem(count, reach, half, size_z),
            vmem(3, count, size_x * reach, size_z),
            vmem(3, count, size_x * reach, size_z),
            vmem(3, count, size_x * reach, size_z),
            vmem(3, count, size_x * reach, size_z),
            vmem(3, pairs, 4 * reach, cells),
            vmem(3, pairs, 4 * reach, cells),
            vmem(sizes[1] * 2, 8, 128),
            vmem(sizes[0] * sizes[2] // 2, 8, 128),
            pltpu.SemaphoreType.DMA((pairs,)),
            pltpu.SemaphoreType.DMA((len(operands) - 1,)),
            pltpu.SemaphoreType.DMA((3, 6)),
            pltpu.SemaphoreType.DMA((3, 6, pairs)),
            pltpu.SemaphoreType.DMA((2,)),
            pltpu.SemaphoreType.DMA((2,)),
        ],
        compiler_params=pltpu.CompilerParams(
            collective_id=0, has_side_effects=True, vmem_limit_bytes=48 << 20
        ),
    )(*(pltpu.with_memory_space_constraint(x, pltpu.HBM) for x in operands))
    return pl.pallas_call(
        finish,
        out_shape=(
            jax.ShapeDtypeStruct(orbitals.shape, f32),
            jax.ShapeDtypeStruct((count, count), f32),
            jax.ShapeDtypeStruct((count, count), f32),
        ),
        in_specs=[whole, whole],
        out_specs=(anywhere, anywhere, anywhere),
        scratch_shapes=[vmem(count, count), vmem(count, count), pltpu.SemaphoreType.DMA((3,))],
        compiler_params=pltpu.CompilerParams(vmem_limit_bytes=8 << 20),
    )(pltpu.with_memory_space_constraint(filtered, pltpu.VMEM), pltpu.with_memory_space_constraint(sums, pltpu.VMEM))


def solution(mesh):
    placed = (P(None, "gx", "gy", "gz"), P("gx", "gy", "gz"))
    return jax.shard_map(
        shards,
        mesh=mesh,
        in_specs=placed,
        out_specs=(P(None, "gx", "gy", "gz"), P(), P()),
        check_vma=False,
    )
```

```python
import functools

import jax
import jax.numpy as jnp
import ml_dtypes
import numpy as np
from jax import lax
from jax.experimental import pallas as pl
from jax.experimental.pallas import tpu as pltpu
from jax.sharding import PartitionSpec as P

MESH = pl.DeviceIdType.MESH
f32, bf16 = jnp.float32, jnp.bfloat16

coefs = (-205.0 / 72.0, 8.0 / 5.0, -1.0 / 5.0, 8.0 / 315.0, -1.0 / 560.0)
reach = 4
kinetic = -0.5 / 0.25
spread = 20.0
middle = 25.0
sigma_one = spread / (-6.0 - middle)
sigma_two = 1.0 / (2.0 / sigma_one - sigma_one)

axes = ("gx", "gy", "gz")
count, size_x, size_y, size_z = 16, 8, 32, 128
pairs = count // 2
cells = size_x * size_y
half = size_y // 2


def two_parts(matrix):
    high = matrix.astype(ml_dtypes.bfloat16)
    low = (matrix - high.astype(np.float64)).astype(ml_dtypes.bfloat16)
    return high, low


def weight(distance):
    return kinetic * coefs[abs(distance)] if 1 <= abs(distance) <= reach else 0.0


def constants():
    along_y = np.zeros((cells, cells))
    faces_y = np.zeros((cells, 2 * size_x * reach))
    for x in range(size_x):
        for y in range(size_y):
            for other in range(size_y):
                along_y[x * size_y + y, x * size_y + other] = weight(other - y)
            for r in range(reach):
                faces_y[x * size_y + y, x * reach + r] = weight(r - reach - y)
                faces_y[x * size_y + y, (size_x + x) * reach + r] = weight(size_y + r - y)
    along_z = np.zeros((size_z, size_z))
    faces_z = np.zeros((4 * reach, 2 * size_z))
    for z in range(size_z):
        for other in range(size_z):
            along_z[other, z] = weight(other - z)
        for r in range(reach):
            for o in range(2):
                faces_z[o * reach + r, o * size_z + z] = weight(r - reach - z)
                faces_z[(2 + o) * reach + r, o * size_z + z] = weight(size_z + r - z)
    pick_z = np.zeros((4 * reach, 2 * size_z))
    for r in range(reach):
        for o in range(2):
            pick_z[o * reach + r, o * size_z + r] = 1.0
            pick_z[(2 + o) * reach + r, o * size_z + size_z - reach + r] = 1.0
    gather = np.zeros((256, 128))
    for j in range(count):
        gather[8 * j : 8 * j + 8, j] = 1.0
        gather[128 + 8 * j : 128 + 8 * j + 8, count + j] = 1.0
    yh, yl = two_parts(along_y)
    fh, fl = two_parts(faces_y)
    zh, zl = two_parts(along_z)
    ch, cl = two_parts(faces_z)
    return (
        np.concatenate([yh, yh, yl], axis=1),
        np.concatenate([fh, fh, fl], axis=1),
        np.concatenate([zh, zh, zl], axis=0),
        np.concatenate([ch, ch, cl], axis=0),
        np.concatenate([pick_z, pick_z], axis=1).astype(ml_dtypes.bfloat16),
        gather.astype(ml_dtypes.bfloat16),
    )


def split(value):
    high = value.astype(bf16)
    return high, (value - high.astype(f32)).astype(bf16)


def dot(left, right, dims=((1,), (0,))):
    return lax.dot_general(left, right, (dims, ((), ())), preferred_element_type=f32)


def kernel(
    scale,
    o_hbm, v_hbm, ay_hbm, fy_hbm, az_hbm, cz_hbm, pick_hbm, gather_hbm,
    out_ref, sum_ref,
    o_ref, v_ref, ay_ref, fy_ref, az_ref, cz_ref, pick_ref, gather_ref,
    first_ref, image_ref, xlo, xhi, xlo3, xhi3, ylo, yhi, ysl, ysh, zr, zs, sum_one, sum_two,
    pair_sem, load_sem, send_sem, recv_sem, sum_send, sum_recv,
):
    def load_pair(c):
        return pltpu.make_async_copy(o_hbm.at[pl.ds(2 * c, 2)], o_ref.at[pl.ds(2 * c, 2)], pair_sem.at[c])

    for c in range(pairs):
        load_pair(c).start()

    sizes = {a: lax.axis_size(a) for a in axes}
    me = {a: lax.axis_index(a) for a in axes}
    right = {a: lax.rem(me[a] + 1, sizes[a]) for a in axes}
    left = {a: lax.rem(me[a] + sizes[a] - 1, sizes[a]) for a in axes}

    def device(x, y, z):
        return (x * sizes["gy"] + y) * sizes["gz"] + z

    inner_z, outer_z = lax.rem(me["gz"], 2), me["gz"] // 2
    outer_size = sizes["gz"] // 2
    def hops(steps, size):
        return min(steps, size - steps)

    near = [
        device(me["gx"], lax.rem(me["gy"] + y, sizes["gy"]), outer_z * 2 + lax.rem(inner_z + z, 2))
        for z in (1, 0) for y in sorted(range(sizes["gy"]), key=lambda y: -hops(y, sizes["gy"])) if y + z
    ]
    far = [
        device(lax.rem(me["gx"] + x, sizes["gx"]), me["gy"], lax.rem(outer_z + z, outer_size) * 2 + inner_z)
        for x, z in sorted(
            ((x, z) for x in range(sizes["gx"]) for z in range(outer_size) if x + z),
            key=lambda xz: -hops(xz[0], sizes["gx"]) - hops(xz[1], outer_size),
        )
    ]
    beside = device(me["gx"], me["gy"], lax.rem(me["gz"] + sizes["gz"] + 2 * inner_z - 1, sizes["gz"]))

    barrier = pltpu.get_barrier_semaphore()
    greeted = near + far + [beside]
    for other in greeted:
        pl.semaphore_signal(barrier, inc=1, device_id=other, device_id_type=pl.DeviceIdType.LOGICAL)
    pl.semaphore_wait(barrier, len(greeted))

    def remote(src, dst, e, way, c, device):
        return pltpu.make_async_remote_copy(
            src_ref=src, dst_ref=dst, send_sem=send_sem.at[e, way], recv_sem=recv_sem.at[e, way, c],
            device_id=device, device_id_type=MESH,
        )

    def x_copies(e, field, two, c):
        if e < 2:
            return (
                remote(field.at[two, 0:reach], xhi.at[e, two], e, 0, c, {"gx": left["gx"]}),
                remote(field.at[two, size_x - reach : size_x], xlo.at[e, two], e, 1, c, {"gx": right["gx"]}),
            )
        return (
            remote(field.at[two, 0:reach, 0:half], xhi3.at[two], e, 0, c, {"gx": left["gx"]}),
            remote(field.at[two, size_x - reach : size_x, half:size_y], xlo3.at[two], e, 1, c, {"gx": right["gx"]}),
        )

    def yz_copies(e, two, one, c):
        low, high = pl.ds(0, 2 * reach), pl.ds(2 * reach, 2 * reach)
        return (
            remote(ysl.at[e, two], yhi.at[e, two], e, 2, c, {"gy": left["gy"]}),
            remote(ysh.at[e, two], ylo.at[e, two], e, 3, c, {"gy": right["gy"]}),
            remote(zs.at[e, one, low], zr.at[e, one, high], e, 4, c, {"gz": left["gz"]}),
            remote(zs.at[e, one, high], zr.at[e, one, low], e, 5, c, {"gz": right["gz"]}),
        )

    def pair(c):
        return pl.ds(2 * c, 2)

    def rows(ref, o):
        return ref[o].reshape(cells, size_z)

    def pack_send(e, field, c):
        for i in range(2):
            o = 2 * c + i
            for x in range(size_x):
                ysl[e, o, x * reach : (x + 1) * reach, :] = field[o, x, 0:reach, :]
                ysh[e, o, x * reach : (x + 1) * reach, :] = field[o, x, size_y - reach : size_y, :]
        h0, l0 = split(rows(field, 2 * c))
        h1, l1 = split(rows(field, 2 * c + 1))
        zs[e, c] = dot(pick_ref[...], jnp.concatenate([h0, h1, l0, l1], axis=1), ((1,), (1,)))
        for copy in yz_copies(e, pair(c), c, c):
            copy.start()

    def inner_yz(field, c):
        h0, l0 = split(rows(field, 2 * c))
        h1, l1 = split(rows(field, 2 * c + 1))
        high, low = jnp.concatenate([h0, h1], axis=1), jnp.concatenate([l0, l1], axis=1)
        y_part = dot(ay_ref[...], jnp.concatenate([high, low, high], axis=0))
        z_part = dot(
            jnp.concatenate(
                [jnp.concatenate([h0, l0, h0], axis=1), jnp.concatenate([h1, l1, h1], axis=1)], axis=0
            ),
            az_ref[...],
        )
        return y_part, z_part

    def faces_yz(e, c):
        around = jnp.concatenate(
            [jnp.concatenate([ylo[e, 2 * c + i], yhi[e, 2 * c + i]], axis=0) for i in range(2)], axis=1
        )
        high, low = split(around)
        y_part = dot(fy_ref[...], jnp.concatenate([high, low, high], axis=0))
        around = zr[e, c]
        high = around.astype(bf16).astype(f32)
        turned = jnp.concatenate([high, around - high, high], axis=0).T.astype(bf16)
        return y_part + dot(turned, cz_ref[...])

    def along_x(get, x):
        total = None
        for k in range(1, reach + 1):
            near = [v for v in (get(x - k), get(x + k)) if v is not None]
            if near:
                term = (near[0] if len(near) == 1 else near[0] + near[1]) * weight(k)
                total = term if total is None else total + term
        return total

    def hamiltonian(e, field, c, shift, write):
        y_part, z_part = inner_yz(field, c)
        around = None if e is None else faces_yz(e, c)
        for i in range(2):
            o = 2 * c + i

            def get(x):
                if x < 0:
                    return None if e is None else xlo[e, o, reach + x]
                if x >= size_x:
                    return None if e is None else xhi[e, o, x - size_x]
                return field[o, x]

            for x in range(size_x):
                block = slice(x * size_y, (x + 1) * size_y)
                lanes = slice(i * size_z, (i + 1) * size_z)
                value = y_part[block, lanes] + z_part[i * cells + x * size_y : i * cells + (x + 1) * size_y]
                if around is not None:
                    value = value + around[block, lanes]
                value = value + along_x(get, x)
                value = value + (v_ref[x] + (3.0 * kinetic * coefs[0] - shift)) * field[o, x]
                write(o, x, value)

    def wait_x(e, field, c):
        for copy in x_copies(e, field, pair(c), c):
            copy.wait_recv()

    def wait_yz(e, c):
        for copy in yz_copies(e, pair(c), c, c):
            copy.wait_recv()

    def each(body):
        lax.fori_loop(0, pairs, lambda c, carry: (body(c), carry)[1], 0)

    def start_first(c):
        load_pair(c).wait()
        for copy in x_copies(0, o_ref, pair(c), c):
            copy.start()

    each(start_first)
    loads = [
        pltpu.make_async_copy(src, dst, load_sem.at[i])
        for i, (src, dst) in enumerate((
            (pick_hbm, pick_ref), (v_hbm, v_ref), (ay_hbm, ay_ref), (fy_hbm, fy_ref),
            (az_hbm, az_ref), (cz_hbm, cz_ref), (gather_hbm, gather_ref),
        ))
    ]
    for load in loads:
        load.start()
    loads[0].wait()
    each(functools.partial(pack_send, 0, o_ref))
    for load in loads[1:]:
        load.wait()

    def step_one(c):
        wait_yz(0, c)
        wait_x(0, o_ref, c)

        def write(o, x, value):
            first_ref[o, x] = value * (sigma_one / spread)

        hamiltonian(0, o_ref, c, middle, write)
        for copy in x_copies(1, first_ref, pair(c), c):
            copy.start()
        pack_send(1, first_ref, c)

    each(step_one)

    def step_two(c):
        wait_yz(1, c)
        wait_x(1, first_ref, c)

        def write(o, x, value):
            out_ref[o, x] = value * (2.0 * sigma_two / spread) - (sigma_one * sigma_two) * o_ref[o, x]

        hamiltonian(1, first_ref, c, middle, write)
        for copy in x_copies(2, out_ref, pair(c), c):
            copy.start()
        pack_send(2, out_ref, c)

        def write_image(o, x, value):
            image_ref[o, x] = value

        hamiltonian(None, out_ref, c, 0.0, write_image)

    def add_faces(c):
        wait_yz(2, c)
        around = faces_yz(2, c)
        for i in range(2):
            o = 2 * c + i
            for x in range(size_x):
                image_ref[o, x] += around[x * size_y : (x + 1) * size_y, i * size_z : (i + 1) * size_z]

    lag = 3

    def step_two_and_faces(c):
        step_two(c)

        @pl.when(c >= lag)
        def _():
            add_faces(c - lag)

    each(step_two_and_faces)
    lax.fori_loop(pairs - lag, pairs, lambda c, carry: (add_faces(c), carry)[1], 0)

    def block(ref, x, tile):
        return split(ref[:, x, tile * 8 : (tile + 1) * 8, :].reshape(8 * count, size_z))

    def rows_dot(left, right):
        return dot(jnp.concatenate(left, axis=1), jnp.concatenate(right, axis=1), ((1,), (1,)))

    def inner_block(x, total):
        for tiles in ((0, 1), (2, 3)):
            left, right = [], []
            for tile in tiles:
                high, low = block(out_ref, x, tile)
                other_high, other_low = block(image_ref, x, tile)
                left.append(jnp.concatenate([high, high, low], axis=1))
                right.append(
                    jnp.concatenate(
                        [
                            jnp.concatenate([high, low, high], axis=1),
                            jnp.concatenate([other_high, other_low, other_high], axis=1),
                        ],
                        axis=0,
                    )
                )
            total = total + rows_dot(left, right)
        return total

    def three_parts(value):
        high, low = split(value)
        rest = (value - high.astype(f32) - low.astype(f32)).astype(bf16)
        return jnp.concatenate([high, low, rest], axis=0)

    def added_up(parts, length):
        return parts[0:length] + parts[length : 2 * length] + parts[2 * length :]

    def collect(total):
        row = lax.broadcasted_iota(jnp.int32, total.shape, 0)
        lane = lax.broadcasted_iota(jnp.int32, total.shape, 1)
        total = jnp.where((row & 7) == (lane & 7), total, 0.0)
        total = total.reshape(count, 8, total.shape[1]).sum(axis=1)
        return added_up(dot(three_parts(total), gather_ref[...]), count)

    inner = lax.fori_loop(0, size_x, inner_block, jnp.zeros((8 * count, 16 * count), f32))
    share = collect(inner)

    def add_cross(c, share):
        sums = [[None, None] for _ in range(count)]
        for x in range(reach):
            from_high = [
                along_x(lambda p: xhi3[2 * c + j, p - size_x] if p >= size_x else None, size_x - reach + x)
                for j in range(2)
            ]
            from_low = [along_x(lambda p: xlo3[2 * c + j, reach + p] if p < 0 else None, x) for j in range(2)]
            for near, layer, begin in ((from_high, size_x - reach + x, 0), (from_low, x, half)):
                for tile in range(0, half, 8):
                    for i in range(count):
                        mine = out_ref[i, layer, begin + tile : begin + tile + 8, :]
                        for j in range(2):
                            term = mine * near[j][tile : tile + 8]
                            sums[i][j] = term if sums[i][j] is None else sums[i][j] + term
        rows = jnp.concatenate(
            [jnp.concatenate([sums[i][j][None] for i in range(count)], axis=0).sum(axis=1) for j in range(2)], axis=0
        )
        rows = added_up(dot(three_parts(rows), jnp.ones((size_z, 128), bf16)), 2 * count)
        lane = lax.broadcasted_iota(jnp.int32, (count, 128), 1)
        for j in range(2):
            share = share + jnp.where(lane == count + 2 * c + j, 2.0 * rows[j * count : (j + 1) * count], 0.0)
        return share

    def two_crosses(c, share):
        wait_x(2, out_ref, 2 * c)
        wait_x(2, out_ref, 2 * c + 1)
        return add_cross(2 * c + 1, add_cross(2 * c, share))

    share = lax.fori_loop(0, pairs // 2, two_crosses, share)
    share = share[0:8] + pltpu.roll(share[8:16], 64, 1)

    stages = (
        (near, sum_one, me["gy"] * 2 + inner_z),
        (far, sum_two, me["gx"] * outer_size + outer_z),
    )
    sent = []
    for position, (others, slots, mine) in enumerate(stages):
        slots[mine] = share

        def sum_copy(ref, other):
            return pltpu.make_async_remote_copy(
                src_ref=ref, dst_ref=ref, send_sem=sum_send.at[position], recv_sem=sum_recv.at[position],
                device_id=other, device_id_type=pl.DeviceIdType.LOGICAL,
            )

        for other in others:
            sum_copy(slots.at[mine], other).start()
        arrived = sum_copy(slots.at[pl.ds(0, len(others))], others[0])
        arrived.wait_recv()
        sent.append(arrived)
        shares = [slots[i] for i in range(len(others) + 1)]
        while len(shares) > 1:
            shares = [shares[i] + shares[i + 1] for i in range(0, len(shares), 2)]
        share = shares[0]

    sum_ref[...] = share * scale

    whole = pl.ds(0, count)
    for e, field in enumerate((o_ref, first_ref, out_ref)):
        for copy in x_copies(e, field, whole, 0) + yz_copies(e, whole, pl.ds(0, pairs), 0):
            copy.wait_send()
    for copy in sent:
        copy.wait_send()


def finish(out_ref, sum_ref, out_hbm, gram_hbm, proj_hbm, gram_ref, proj_ref, sems):
    move = pltpu.make_async_copy(out_ref, out_hbm, sems.at[0])
    move.start()
    total = jnp.concatenate([sum_ref[...], pltpu.roll(sum_ref[...], 64, 1)], axis=0)
    turned = total.T
    gram_ref[...] = total[:, 0:count]
    proj_ref[...] = 0.5 * (total[:, count : 2 * count] + turned[count : 2 * count, :])
    moves = [
        move,
        pltpu.make_async_copy(gram_ref, gram_hbm, sems.at[1]),
        pltpu.make_async_copy(proj_ref, proj_hbm, sems.at[2]),
    ]
    for later in moves[1:]:
        later.start()
    for each in moves:
        each.wait()


def shards(orbitals, potential):
    sizes = [lax.axis_size(a) for a in axes]
    total = cells * size_z * sizes[0] * sizes[1] * sizes[2]
    operands = (orbitals, potential, *(jnp.asarray(c) for c in constants()))
    vmem = lambda *shape: pltpu.VMEM(shape, f32)
    whole, anywhere = pl.BlockSpec(memory_space=pltpu.VMEM), pl.BlockSpec(memory_space=pltpu.HBM)
    filtered, sums = pl.pallas_call(
        functools.partial(kernel, 1.0 / total),
        out_shape=(vmem(*orbitals.shape), vmem(8, 128)),
        in_specs=[anywhere] * len(operands),
        out_specs=(whole, whole),
        scratch_shapes=[
            *(pltpu.VMEM(x.shape, x.dtype) for x in operands),
            vmem(count, size_x, size_y, size_z),
            vmem(count, size_x, size_y, size_z),
            vmem(2, count, reach, size_y, size_z),
            vmem(2, count, reach, size_y, size_z),
            vmem(count, reach, half, size_z),
            vmem(count, reach, half, size_z),
            vmem(3, count, size_x * reach, size_z),
            vmem(3, count, size_x * reach, size_z),
            vmem(3, count, size_x * reach, size_z),
            vmem(3, count, size_x * reach, size_z),
            vmem(3, pairs, 4 * reach, cells),
            vmem(3, pairs, 4 * reach, cells),
            vmem(sizes[1] * 2, 8, 128),
            vmem(sizes[0] * sizes[2] // 2, 8, 128),
            pltpu.SemaphoreType.DMA((pairs,)),
            pltpu.SemaphoreType.DMA((len(operands) - 1,)),
            pltpu.SemaphoreType.DMA((3, 6)),
            pltpu.SemaphoreType.DMA((3, 6, pairs)),
            pltpu.SemaphoreType.DMA((2,)),
            pltpu.SemaphoreType.DMA((2,)),
        ],
        compiler_params=pltpu.CompilerParams(
            collective_id=0, has_side_effects=True, vmem_limit_bytes=48 << 20
        ),
    )(*(pltpu.with_memory_space_constraint(x, pltpu.HBM) for x in operands))
    return pl.pallas_call(
        finish,
        out_shape=(
            jax.ShapeDtypeStruct(orbitals.shape, f32),
            jax.ShapeDtypeStruct((count, count), f32),
            jax.ShapeDtypeStruct((count, count), f32),
        ),
        in_specs=[whole, whole],
        out_specs=(anywhere, anywhere, anywhere),
        scratch_shapes=[vmem(count, count), vmem(count, count), pltpu.SemaphoreType.DMA((3,))],
        compiler_params=pltpu.CompilerParams(vmem_limit_bytes=8 << 20),
    )(pltpu.with_memory_space_constraint(filtered, pltpu.VMEM), pltpu.with_memory_space_constraint(sums, pltpu.VMEM))


def solution(mesh):
    placed = (P(None, "gx", "gy", "gz"), P("gx", "gy", "gz"))
    return jax.shard_map(
        shards,
        mesh=mesh,
        in_specs=placed,
        out_specs=(P(None, "gx", "gy", "gz"), P(), P()),
        check_vma=False,
    )
```
